512 devices in a mesh: pair: 64 (over z, y), tile: 8 (over x, core).
Axes of the slice: x: 4, y: 4, z: 16, core: 2. Of those that a mesh axis runs over, the one named last changes fastest.
Arguments:
- candidates: bfloat16 [131072, 768], P(('pair', 'tile')), may hold values from -12 to 12, as said below
- validation: bfloat16 [8192, 768], P('tile'), may hold values from -12 to 12, as said below
- row_sizes: int32 [16], replicated, may hold values from 1024 to 24576, as said below
- col_sizes: int32 [16], replicated, may hold values from 1 to 1536, 8192 in all
Outputs:
- row_value: float32 [131072], P(('pair', 'tile'))
- col_potential: float32 [8192], P('tile')
The draws below stay inside these ranges and needn't reach their ends.
Inputs may be any that keep to these rules, and one draw needn't show every extreme that they name: `candidates`: each row's entries are drawn alike and scaled by one factor of the row. `validation`: each row's entries are drawn alike and scaled by one factor of the row. `row_sizes`: every domain pair has 1024 rows or more; one pair has exactly 1024 rows and one exactly 24576.
All inputs are finite; a program needn't handle non-finite values.
Results may differ from the reference program's by a relative error of at most 0.0003.
Values may be sent and summed in bfloat16 or wider, within the bound.
A program may use at most 192 MiB of HBM per device.

```python
import math
import jax
import jax.numpy as jnp
import numpy as np
from jax import lax

D = 768
PAIRS = 16
ITERS = 3
ROWS = 131072
COLS = 8192
ROW_MOST = 24576
ROW_LEAST = 1024
COL_MOST = 1536


def scaled_rows(key, count):
    entry_key = jax.random.fold_in(key, 11)
    scale_key = jax.random.fold_in(key, 23)
    entries = jnp.clip(jax.random.normal(entry_key, (count, D), jnp.float32), -6.0, 6.0)
    scales = jnp.exp(jax.random.uniform(scale_key, (count, 1), jnp.float32, math.log(0.5), math.log(2.0)))
    return (entries * scales).astype(jnp.bfloat16)


def draw_candidates(key, part):
    return scaled_rows(key, ROWS)


def draw_validation(key, part):
    return scaled_rows(key, COLS)


def draw_row_sizes(key, part):
    order_key = jax.random.fold_in(key, 37)
    weight_key = jax.random.fold_in(key, 41)
    order = jax.random.permutation(order_key, jnp.arange(PAIRS, dtype=jnp.int32))
    ranks = jnp.arange(PAIRS, dtype=jnp.int32)
    weights = jax.random.randint(weight_key, (PAIRS,), 1, 4, dtype=jnp.int32)
    weights = jnp.where(ranks < 2, 0, weights)
    spare = ROWS - ROW_MOST - (PAIRS - 1) * ROW_LEAST
    extra = spare * weights // jnp.sum(weights)
    left = spare - jnp.sum(extra)
    extra = extra + ((ranks >= 2) & (ranks < 2 + left)).astype(jnp.int32)
    by_rank = jnp.where(ranks == 0, ROW_MOST, ROW_LEAST + extra).astype(jnp.int32)
    return jnp.zeros((PAIRS,), jnp.int32).at[order].set(by_rank)


def profile(amount, total, limit, lean):
    portions = [(1 << 20) // math.isqrt(grade ** lean) + 1 for grade in range(2, amount + 1)]
    surplus, holding = total - limit - (amount - 1), [1] * (amount - 1)
    while surplus > 0:
        free = [i for i in range(amount - 1) if holding[i] < limit]
        pool, budget = sum([portions[i] for i in free]), surplus
        for i in free:
            addition = min(limit - holding[i], max(1, budget * portions[i] // pool), surplus)
            holding[i] = holding[i] + addition
            surplus = surplus - addition
    return np.array([limit] + holding)


def uneven(key, count, total, bound, slope):
    if count == 2:
        one = jax.random.randint(key, (), max(1, total - bound), min(bound, total - 1) + 1)
        return jnp.stack([one, total - one])
    sizes = jnp.asarray(profile(count, total, bound, slope), jnp.int32)
    twos = (count - 1) // 2
    donor, sink = sizes[1:1 + 2 * twos:2], sizes[2:2 + 2 * twos:2]
    slack = jnp.minimum(donor - 1, bound - sink)
    shifted = jax.random.randint(jax.random.fold_in(key, 1), (twos,), 0, 1 << 20) % (slack + 1)
    sizes = sizes.at[1:1 + 2 * twos:2].set(donor - shifted).at[2:2 + 2 * twos:2].set(sink + shifted)
    return sizes[jax.random.permutation(jax.random.fold_in(key, 2), count)]


def setup_inputs(seed: int = 0) -> dict:
    seeds = jax.random.split(jax.random.key(seed), 5)
    return {
        "candidates": draw_candidates(jax.random.fold_in(seeds[4], 71), 0),
        "validation": draw_validation(jax.random.fold_in(seeds[4], 71), 0),
        "row_sizes": draw_row_sizes(jax.random.fold_in(seeds[4], 71), 0),
        "col_sizes": uneven(seeds[3], PAIRS, COLS, COL_MOST, 2).astype(jnp.int32),
    }


EPS = 0.02
NEG = -1.0e30


def pair_ids(sizes, count):
    ends = jnp.cumsum(sizes)
    positions = jnp.arange(count, dtype=jnp.int32)
    return jnp.sum((positions[:, None] >= ends[None, :]).astype(jnp.int32), axis=1).astype(jnp.int32)


def reference(candidates, validation, row_sizes, col_sizes):
    row_pair = pair_ids(row_sizes, ROWS)
    col_pair = pair_ids(col_sizes, COLS)
    row_table = EPS * jnp.log(row_sizes.astype(jnp.float32))
    col_table = EPS * jnp.log(col_sizes.astype(jnp.float32))
    valid_f = validation.astype(jnp.float32)
    col_norm = jnp.sum(valid_f * valid_f, axis=1)
    block = math.gcd(ROWS, 1024)
    blocks = ROWS // block
    cand_blocks = candidates.reshape(blocks, block, D)
    pair_blocks = row_pair.reshape(blocks, block)

    def block_cost(rows):
        rows_f = rows.astype(jnp.float32)
        row_norm = jnp.sum(rows_f * rows_f, axis=1)
        cross = jnp.dot(rows, validation.T, preferred_element_type=jnp.float32)
        return (row_norm[:, None] + col_norm[None, :] - 2.0 * cross) / D

    cost = lax.map(block_cost, cand_blocks)
    potential_g = jnp.zeros((COLS,), jnp.float32)
    potential_f = jnp.zeros((blocks, block), jnp.float32)
    for step in range(ITERS):
        def f_block(args):
            tile_cost, pairs = args
            mask = pairs[:, None] == col_pair[None, :]
            scores = jnp.where(mask, (potential_g[None, :] - tile_cost) / EPS, NEG)
            top = jnp.max(scores, axis=1)
            total = jnp.sum(jnp.where(mask, jnp.exp(scores - top[:, None]), 0.0), axis=1)
            return -EPS * (top + jnp.log(total)) + col_table[pairs]

        potential_f = lax.map(f_block, (cost, pair_blocks))

        def g_step(carry, args):
            top_old, total_old = carry
            tile_cost, pairs, fvals = args
            mask = pairs[:, None] == col_pair[None, :]
            scores = jnp.where(mask, (fvals[:, None] - tile_cost) / EPS, NEG)
            top_new = jnp.max(scores, axis=0)
            total_new = jnp.sum(jnp.where(mask, jnp.exp(scores - top_new[None, :]), 0.0), axis=0)
            top = jnp.maximum(top_old, top_new)
            total = total_old * jnp.exp(top_old - top) + total_new * jnp.exp(top_new - top)
            return (top, total), None

        start = (jnp.full((COLS,), NEG, jnp.float32), jnp.zeros((COLS,), jnp.float32))
        (top, total), unused = lax.scan(g_step, start, (cost, pair_blocks, potential_f))
        potential_g = -EPS * (top + jnp.log(total)) + row_table[col_pair]
    flat_f = potential_f.reshape(ROWS)
    sums = jax.ops.segment_sum(flat_f, row_pair, num_segments=PAIRS)
    means = sums / row_sizes.astype(jnp.float32)
    row_value = flat_f - means[row_pair]
    return row_value, potential_g
```

```python
import functools
import math

import jax
import jax.numpy as jnp
from jax import lax
from jax.experimental import pallas as pl
from jax.experimental.pallas import tpu as pltpu
from jax.sharding import PartitionSpec as P

ITERS = 3
EPS = 0.02
NEG = -1e30
EMPTY = -1e29
LOG2E = math.log2(math.e)
NX, NY = 4, 4
TILES = 2 * NX
ROW_MOST = 24576
LANES = 128
MESH = pl.DeviceIdType.MESH


def pair_of(position, ends):
    pair = jnp.zeros(position.shape, jnp.int32)
    for end in ends:
        pair += (position >= end).astype(jnp.int32)
    return pair


def size_of(pair, sizes):
    size = jnp.zeros(pair.shape, jnp.float32)
    for k, s in enumerate(sizes):
        size = jnp.where(pair == k, s.astype(jnp.float32), size)
    return size


def merged(parts):
    top = jnp.max(parts, axis=0)
    return top + jnp.log2(jnp.sum(jnp.exp2(parts - top[None]), axis=0))


def kernel(
    pair_count,
    group_count,
    rs_ref,
    cs_ref,
    x_ref,
    y_ref,
    f_ref,
    g_ref,
    rows,
    scores,
    v_wide,
    pair_wide,
    top_wide,
    cn,
    column,
    row_box,
    y_box,
    z_box,
    local_sem,
    send_sem,
    block_sem,
    row_sem,
    y_sem,
    z_sem,
):
    n_row, depth = x_ref.shape
    n_col = y_ref.shape[0]
    half = n_row // 2
    halves = 2 * TILES
    col_blocks = n_col // LANES
    nz = group_count // NY
    window = min(-(-ROW_MOST // (n_row * TILES * NY)), nz // 2)
    scale = 2.0 * LOG2E / (depth * EPS)
    shift = LOG2E / (depth * EPS)

    group = lax.axis_index("pair")
    tile = lax.axis_index("tile")
    z, y = group // NY, lax.rem(group, NY)
    x, core = tile // 2, lax.rem(tile, 2)

    def at(dx, flip):
        other = 1 - core if flip else core
        return 2 * lax.rem(x + dx, NX) + other

    def in_y(r):
        return z * NY + lax.rem(y + r, NY)

    def in_z(r):
        return lax.rem(z + r, nz) * NY + y

    with jax.named_scope("greet"):
        own_copy = pltpu.make_async_copy(x_ref, rows.at[tile], local_sem)
        own_copy.start()
        barrier = pltpu.get_barrier_semaphore()
        for r in range(1, TILES):
            pl.semaphore_signal(
                barrier, device_id=(group, lax.rem(tile + r, TILES)), device_id_type=MESH
            )
        for r in range(1, NY):
            pl.semaphore_signal(barrier, device_id=(in_y(r), tile), device_id_type=MESH)
        for r in range(1, nz):
            pl.semaphore_signal(barrier, device_id=(in_z(r), tile), device_id_type=MESH)

    row_ends, col_ends = [], []
    row_sizes, col_sizes = [], []
    for k in range(pair_count):
        row_sizes.append(rs_ref[k])
        col_sizes.append(cs_ref[k])
        row_ends.append(row_sizes[k] + (row_ends[-1] if k else 0))
        col_ends.append(col_sizes[k] + (col_ends[-1] if k else 0))

    lane = lax.broadcasted_iota(jnp.int32, (LANES, LANES), 1)
    line = lax.broadcasted_iota(jnp.int32, (LANES, LANES), 0)
    eye = lane == line

    def flat(tall):
        return jnp.sum(jnp.where(eye, tall, 0.0), axis=0, keepdims=True)

    def tall(flat_row):
        spread = jnp.where(eye, jnp.broadcast_to(flat_row, (LANES, LANES)), 0.0)
        return jnp.broadcast_to(jnp.sum(spread, axis=1, keepdims=True), (LANES, LANES))

    def squares(block):
        wide = block.astype(jnp.float32)
        total = jnp.sum(wide * wide, axis=1, keepdims=True)
        return jnp.broadcast_to(total, (LANES, LANES))

    with jax.named_scope("column_norms"):

        def column_block(q, carry):
            span = pl.ds(pl.multiple_of(q * LANES, LANES), LANES)
            norm = squares(y_ref[span, :])
            v_wide[span, :] = -shift * norm
            cn[pl.ds(q, 1), :] = flat(norm)
            pair_wide[span, :] = pair_of(tile * n_col + q * LANES + line, col_ends)
            return carry

        lax.fori_loop(0, col_blocks, column_block, 0)

    with jax.named_scope("greeted"):
        pl.semaphore_wait(barrier, TILES - 1 + NY - 1 + nz - 1)
        own_copy.wait()

    def send_block(block, part, to, sem):
        ref = rows.at[block, pl.ds(part * half, half)]
        copy = pltpu.make_async_remote_copy(
            src_ref=ref,
            dst_ref=ref,
            send_sem=send_sem.at[0],
            recv_sem=block_sem.at[sem, part],
            device_id=(group, to),
            device_id_type=MESH,
        )
        copy.start()

    def wait_half(sem, part):
        ref = rows.at[0, pl.ds(0, half)]
        pltpu.make_async_copy(ref, ref, block_sem.at[sem, part]).wait()

    SIB, LEFT, RIGHT, LEFT_SIB, RIGHT_SIB, OPP, OPP_SIB = range(7)
    right, left, sib = at(1, False), at(NX - 1, False), at(0, True)

    with jax.named_scope("send_own"):
        send_block(tile, 0, right, LEFT)
        send_block(tile, 1, left, RIGHT)
        send_block(tile, 1, right, LEFT)
        send_block(tile, 0, left, RIGHT)
        send_block(tile, 0, sib, SIB)
        send_block(tile, 1, sib, SIB)

    row_box[0, tile] = jnp.zeros(row_box.shape[2:], jnp.float32)
    for h in range(2):
        row_box[0, tile, pl.ds(halves + h, 1), :] = flat(
            squares(rows[tile, pl.ds(h * half, half), :])
        )

    chunk = min(512, n_col)

    def score_block(block):
        first = group * (n_row * TILES) + block * n_row
        block_pair = [
            pair_of(first + h * half + lane[:1], row_ends) for h in range(2)
        ]

        def product(i, top):
            span = pl.ds(pl.multiple_of(i * chunk, chunk), chunk)
            cross = lax.dot_general(
                y_ref[span, :],
                rows[block],
                (((1,), (1,)), ((), ())),
                preferred_element_type=jnp.float32,
            )
            v = v_wide[span, :]
            col_pair = pair_wide[span, :]
            new = []
            for h in range(2):
                k = jnp.where(
                    col_pair == block_pair[h], cross[:, h * half : (h + 1) * half] * scale, NEG
                )
                scores[2 * block + h, span, :] = k
                new.append(
                    jnp.maximum(top[h], jnp.max((k + v).reshape(chunk // 8, 8, LANES), axis=0))
                )
            return tuple(new)

        start = jnp.full((8, LANES), 4 * NEG, jnp.float32)
        top = lax.fori_loop(0, n_col // chunk, product, (start, start))
        top = [jnp.max(t, axis=0, keepdims=True) for t in top]

        def total(i, so_far):
            span = pl.ds(pl.multiple_of(i * LANES, LANES), LANES)
            v = v_wide[span, :]
            new = []
            for h in range(2):
                e = jnp.exp2(scores[2 * block + h, span, :] + v - top[h])
                new.append(so_far[h] + jnp.sum(e.reshape(LANES // 8, 8, LANES), axis=0))
            return tuple(new)

        start = jnp.zeros((8, LANES), jnp.float32)
        sums = lax.fori_loop(0, n_col // LANES, total, (start, start))
        for h in range(2):
            row_box[0, tile, pl.ds(2 * block + h, 1), :] = top[h] + jnp.log2(
                jnp.sum(sums[h], axis=0, keepdims=True)
            )

    def score_blocks(dx, flip):
        score_block(at(dx, flip))

    with jax.named_scope("scores_near"):
        score_blocks(0, False)
        wait_half(SIB, 0)
        wait_half(SIB, 1)
        score_blocks(0, True)

    left_block, right_block = at(NX - 1, False), at(1, False)
    opposite = at(2, False)
    with jax.named_scope("forward"):
        wait_half(LEFT, 0)
        send_block(left_block, 0, right, OPP)
        send_block(left_block, 0, sib, LEFT_SIB)
        wait_half(RIGHT, 1)
        send_block(right_block, 1, left, OPP)
        send_block(right_block, 1, sib, RIGHT_SIB)
        wait_half(LEFT, 1)
        send_block(left_block, 1, sib, LEFT_SIB)
        wait_half(RIGHT, 0)
        send_block(right_block, 0, sib, RIGHT_SIB)

    with jax.named_scope("scores_sides"):

        def side(s, carry):
            score_block(2 * lax.rem(x + 1 + 2 * s, NX) + core)
            return carry

        lax.fori_loop(0, 2, side, 0)
        for part in range(2):
            wait_half(LEFT_SIB, part)
            wait_half(RIGHT_SIB, part)

        def other_side(s, carry):
            score_block(2 * lax.rem(x + 1 + 2 * s, NX) + 1 - core)
            return carry

        lax.fori_loop(0, 2, other_side, 0)

    with jax.named_scope("wait_opposite"):
        for part in range(2):
            wait_half(OPP, part)
            send_block(opposite, part, sib, OPP_SIB)
    with jax.named_scope("scores_opposite"):
        score_blocks(2, False)
        for part in range(2):
            wait_half(OPP_SIB, part)
        score_blocks(2, True)

    row_line = lax.broadcasted_iota(jnp.int32, (halves, LANES), 0)
    row_lane = lax.broadcasted_iota(jnp.int32, (halves, LANES), 1)
    row_pair = pair_of(group * (n_row * TILES) + row_line * half + row_lane, row_ends)
    log_cs = jnp.log2(size_of(row_pair, col_sizes))
    col_line = lax.broadcasted_iota(jnp.int32, (col_blocks, LANES), 0)
    col_lane = lax.broadcasted_iota(jnp.int32, (col_blocks, LANES), 1)
    col_pair = pair_of(tile * n_col + col_line * LANES + col_lane, col_ends)
    log_rs = jnp.log2(size_of(col_pair, row_sizes))

    def row_pass(step):
        def highest(i, top):
            span = pl.ds(pl.multiple_of(i * 8, 8), 8)
            return jnp.maximum(top, scores[:, span, :] + v_wide[span, :][None])

        start = jnp.full((halves, 8, LANES), 4 * NEG, jnp.float32)
        top = lax.fori_loop(0, n_col // 8, highest, start, unroll=4)
        top = jnp.max(top, axis=1)

        def total(i, so_far):
            span = pl.ds(pl.multiple_of(i * 8, 8), 8)
            return so_far + jnp.exp2(scores[:, span, :] + v_wide[span, :][None] - top[:, None, :])

        start = jnp.zeros((halves, 8, LANES), jnp.float32)
        sums = lax.fori_loop(0, n_col // 8, total, start, unroll=4)
        row_box[step, tile, :halves, :] = top + jnp.log2(jnp.sum(sums, axis=1))

    def column_pass(u):
        u_wide = u[:, None, :]

        def highest(i, carry):
            span = pl.ds(pl.multiple_of(i * 8, 8), 8)
            top = jnp.max(scores[:, span, :] + u_wide, axis=0)
            top_wide[span, :] = jnp.broadcast_to(jnp.max(top, axis=1, keepdims=True), (8, LANES))
            return carry

        lax.fori_loop(0, n_col // 8, highest, 0, unroll=4)

        def total(i, carry):
            span = pl.ds(pl.multiple_of(i * 8, 8), 8)
            top = top_wide[span, :]
            e = jnp.sum(jnp.exp2(scores[:, span, :] + u_wide - top[None]), axis=0)
            lse = top + jnp.log2(jnp.sum(e, axis=1, keepdims=True))
            top_wide[span, :] = jnp.broadcast_to(lse, (8, LANES))
            return carry

        lax.fori_loop(0, n_col // 8, total, 0, unroll=4)
        for q in range(col_blocks):
            column[pl.ds(q, 1), :] = flat(top_wide[pl.ds(q * LANES, LANES), :])
        return column[...]

    def share(box, step, me, size, targets, send, recv):
        slot = box.at[step, me, pl.ds(0, size)]
        for to in targets:
            pltpu.make_async_remote_copy(
                src_ref=slot,
                dst_ref=slot,
                send_sem=send,
                recv_sem=recv,
                device_id=to,
                device_id_type=MESH,
            ).start()
        some = box.at[step, pl.ds(0, len(targets)), pl.ds(0, size)]
        pltpu.make_async_copy(some, some, recv).wait()

    def sent(box, step, count, size, send):
        some = box.at[step, pl.ds(0, count), pl.ds(0, size)]
        pltpu.make_async_copy(some, some, send).wait()

    z_targets = []
    for step in range(ITERS):
        last = step + 1 == ITERS
        if step:
            with jax.named_scope("row_pass"):
                row_pass(step)
        with jax.named_scope("row_share"):
            share(
                row_box,
                step,
                tile,
                row_box.shape[2] if step == 0 else halves,
                [(group, lax.rem(tile + r, TILES)) for r in range(1, TILES)],
                send_sem.at[1 + 3 * step],
                row_sem.at[step],
            )
            u = log_cs - merged(row_box[step, :, :halves, :])
        with jax.named_scope("column_pass"):
            y_box[step, y, :col_blocks, :] = column_pass(u)
        size = col_blocks
        if last:
            size = col_blocks + pair_count
            f = (EPS / LOG2E) * u
            f = f + jnp.concatenate(
                [row_box[0, t, halves : halves + 2, :] for t in range(TILES)], axis=0
            ) * (1.0 / depth)
            for k in range(pair_count):
                y_box[step, y, pl.ds(col_blocks + k, 1), :] = jnp.sum(
                    jnp.where(row_pair == k, f, 0.0), axis=0, keepdims=True
                )
        with jax.named_scope("column_share_y"):
            share(
                y_box,
                step,
                y,
                size,
                [(in_y(r), tile) for r in range(1, NY)],
                send_sem.at[2 + 3 * step],
                y_sem.at[step],
            )
            lse = merged(y_box[step, :, :col_blocks, :])
            z_box[step, z, :col_blocks, :] = lse
            if last:
                z_box[step, z, col_blocks:, :] = jnp.sum(y_box[step, :, col_blocks:, :], axis=0)
        with jax.named_scope("column_share_z"):
            if last:
                near = list(range(1, nz))
            else:
                near = sorted({r % nz for r in range(-window, window + 1)} - {0})
            z_targets.append(len(near))
            if len(near) < nz - 1:
                for r in range(1, nz):
                    if r not in near:
                        z_box[step, lax.rem(z + r, nz), :col_blocks, :] = jnp.full(
                            (col_blocks, LANES), NEG, jnp.float32
                        )
            share(
                z_box,
                step,
                z,
                size,
                [(in_z(r), tile) for r in near],
                send_sem.at[3 + 3 * step],
                z_sem.at[step],
            )
            lse = merged(z_box[step, :, :col_blocks, :])
            v = jnp.where(lse > EMPTY, log_rs - lse, 0.0)
        if not last:
            with jax.named_scope("spread"):
                for q in range(col_blocks):
                    v_wide[pl.ds(q * LANES, LANES), :] = tall(v[q : q + 1, :])

    with jax.named_scope("results"):
        g_ref[...] = (EPS / LOG2E) * v + cn[...] * (1.0 / depth)
        sums = jnp.sum(z_box[ITERS - 1, :, col_blocks:, :], axis=0)
        sums = jnp.broadcast_to(jnp.sum(sums, axis=1, keepdims=True), (pair_count, LANES))
        value = jnp.zeros((2, LANES), jnp.float32)
        own_pair = jnp.zeros((2, LANES), jnp.int32)
        for t in range(TILES):
            value = jnp.where(tile == t, f[2 * t : 2 * t + 2], value)
            own_pair = jnp.where(tile == t, row_pair[2 * t : 2 * t + 2], own_pair)
        mean = jnp.zeros((2, LANES), jnp.float32)
        for k in range(pair_count):
            mean = jnp.where(own_pair == k, sums[k : k + 1, :], mean)
        f_ref[...] = value - mean / size_of(own_pair, row_sizes)

    with jax.named_scope("sent"):
        ref = rows.at[pl.ds(0, 7)]
        pltpu.make_async_copy(ref, ref, send_sem.at[0]).wait()
        for step in range(ITERS):
            last = step + 1 == ITERS
            width = row_box.shape[2] if step == 0 else halves
            size = col_blocks + (pair_count if last else 0)
            sent(row_box, step, TILES - 1, width, send_sem.at[1 + 3 * step])
            sent(y_box, step, NY - 1, size, send_sem.at[2 + 3 * step])
            sent(z_box, step, z_targets[step], size, send_sem.at[3 + 3 * step])


def local(candidates, validation, row_sizes, col_sizes):
    groups = lax.axis_size("pair")
    n_row, depth = candidates.shape
    n_col = validation.shape[0]
    pairs = row_sizes.shape[0]
    halves = 2 * TILES
    half = n_row // 2
    col_blocks = n_col // LANES
    vmem = pl.BlockSpec(memory_space=pltpu.VMEM)
    smem = pl.BlockSpec(memory_space=pltpu.SMEM)
    row_value, col_potential = pl.pallas_call(
        functools.partial(kernel, pairs, groups),
        out_shape=(
            jax.ShapeDtypeStruct((2, half), jnp.float32),
            jax.ShapeDtypeStruct((col_blocks, LANES), jnp.float32),
        ),
        in_specs=[smem, smem, vmem, vmem],
        out_specs=(vmem, vmem),
        scratch_shapes=[
            pltpu.VMEM((TILES, n_row, depth), jnp.bfloat16),
            pltpu.VMEM((halves, n_col, half), jnp.float32),
            pltpu.VMEM((n_col, LANES), jnp.float32),
            pltpu.VMEM((n_col, LANES), jnp.int32),
            pltpu.VMEM((n_col, LANES), jnp.float32),
            pltpu.VMEM((col_blocks, LANES), jnp.float32),
            pltpu.VMEM((col_blocks, LANES), jnp.float32),
            pltpu.VMEM((ITERS, TILES, halves + 8, half), jnp.float32),
            pltpu.VMEM((ITERS, NY, col_blocks + pairs, LANES), jnp.float32),
            pltpu.VMEM((ITERS, groups // NY, col_blocks + pairs, LANES), jnp.float32),
            pltpu.SemaphoreType.DMA,
            pltpu.SemaphoreType.DMA((1 + 3 * ITERS,)),
            pltpu.SemaphoreType.DMA((7, 2)),
            pltpu.SemaphoreType.DMA((ITERS,)),
            pltpu.SemaphoreType.DMA((ITERS,)),
            pltpu.SemaphoreType.DMA((ITERS,)),
        ],
        compiler_params=pltpu.CompilerParams(
            collective_id=0, has_side_effects=True, vmem_limit_bytes=48 * 2**20
        ),
    )(row_sizes, col_sizes, candidates, validation)
    return row_value.reshape(n_row), col_potential.reshape(n_col)


def solution(mesh):
    in_specs = (P(("pair", "tile"), None), P("tile", None), P(), P())
    out_specs = (P(("pair", "tile")), P("tile"))
    return jax.shard_map(local, mesh=mesh, in_specs=in_specs, out_specs=out_specs, check_vma=False)
```

```python
import functools
import math

import jax
import jax.numpy as jnp
from jax import lax
from jax.experimental import pallas as pl
from jax.experimental.pallas import tpu as pltpu
from jax.sharding import PartitionSpec as P

ITERS = 3
EPS = 0.02
NEG = -1e30
EMPTY = -1e29
LOG2E = math.log2(math.e)
NX, NY = 4, 4
TILES = 2 * NX
ROW_MOST = 24576
LANES = 128
MESH = pl.DeviceIdType.MESH


def pair_of(position, ends):
    pair = jnp.zeros(position.shape, jnp.int32)
    for end in ends:
        pair += (position >= end).astype(jnp.int32)
    return pair


def size_of(pair, sizes):
    size = jnp.zeros(pair.shape, jnp.float32)
    for k, s in enumerate(sizes):
        size = jnp.where(pair == k, s.astype(jnp.float32), size)
    return size


def merged(parts):
    top = jnp.max(parts, axis=0)
    return top + jnp.log2(jnp.sum(jnp.exp2(parts - top[None]), axis=0))


def kernel(
    pair_count,
    group_count,
    rs_hbm,
    cs_hbm,
    x_ref,
    y_hbm,
    f_ref,
    g_ref,
    rs_ref,
    cs_ref,
    y_ref,
    rows,
    scores,
    v_wide,
    pair_wide,
    top_wide,
    sum_wide,
    cn,
    column,
    row_box,
    near_box,
    y_box,
    z_box,
    local_sem,
    send_sem,
    block_sem,
    row_sem,
    near_sem,
    y_sem,
    z_sem,
):
    n_row, depth = x_ref.shape
    n_col = y_ref.shape[0]
    half = n_row // 2
    halves = 2 * TILES
    col_blocks = n_col // LANES
    nz = group_count // NY
    reach = -(-ROW_MOST // (n_row * TILES))
    scale = 2.0 * LOG2E / (depth * EPS)
    shift = LOG2E / (depth * EPS)

    group = lax.axis_index("pair")
    tile = lax.axis_index("tile")
    z, y = group // NY, lax.rem(group, NY)
    x, core = tile // 2, lax.rem(tile, 2)

    def at(dx, flip):
        other = 1 - core if flip else core
        return 2 * lax.rem(x + dx, NX) + other

    def in_y(r):
        return z * NY + lax.rem(y + r, NY)

    def in_z(r):
        return lax.rem(z + r, nz) * NY + y

    with jax.named_scope("greet"):
        near = [(lax.rem(group + r + group_count, group_count), tile) for r in range(-reach, reach + 1) if r]
        copies = [
            pltpu.make_async_copy(a, b, local_sem.at[i])
            for i, (a, b) in enumerate(
                [(x_ref, rows.at[tile]), (rs_hbm, rs_ref), (cs_hbm, cs_ref), (y_hbm, y_ref)]
            )
        ]
        for copy in copies:
            copy.start()
        barrier = pltpu.get_barrier_semaphore()
        for r in range(1, TILES):
            pl.semaphore_signal(
                barrier, device_id=(group, lax.rem(tile + r, TILES)), device_id_type=MESH
            )
        for to in near:
            pl.semaphore_signal(barrier, device_id=to, device_id_type=MESH)
        copies[0].wait()
        pl.semaphore_wait(barrier, TILES - 1 + len(near))

    def send_block(block, part, to, sem):
        ref = rows.at[block, pl.ds(part * half, half)]
        copy = pltpu.make_async_remote_copy(
            src_ref=ref,
            dst_ref=ref,
            send_sem=send_sem.at[0],
            recv_sem=block_sem.at[sem, part],
            device_id=(group, to),
            device_id_type=MESH,
        )
        copy.start()

    def wait_half(sem, part):
        ref = rows.at[0, pl.ds(0, half)]
        pltpu.make_async_copy(ref, ref, block_sem.at[sem, part]).wait()

    SIB, LEFT, RIGHT, LEFT_SIB, RIGHT_SIB, OPP, OPP_SIB = range(7)
    right, left, sib = at(1, False), at(NX - 1, False), at(0, True)

    with jax.named_scope("send_own"):
        send_block(tile, 0, right, LEFT)
        send_block(tile, 1, left, RIGHT)
        send_block(tile, 1, right, LEFT)
        send_block(tile, 0, left, RIGHT)
        send_block(tile, 0, sib, SIB)
        send_block(tile, 1, sib, SIB)

    with jax.named_scope("inputs"):
        for copy in copies[1:]:
            copy.wait()

    row_ends, col_ends = [], []
    row_sizes, col_sizes = [], []
    for k in range(pair_count):
        row_sizes.append(rs_ref[k])
        col_sizes.append(cs_ref[k])
        row_ends.append(row_sizes[k] + (row_ends[-1] if k else 0))
        col_ends.append(col_sizes[k] + (col_ends[-1] if k else 0))

    lane = lax.broadcasted_iota(jnp.int32, (LANES, LANES), 1)
    line = lax.broadcasted_iota(jnp.int32, (LANES, LANES), 0)
    eye = lane == line

    def flat(tall):
        return jnp.sum(jnp.where(eye, tall, 0.0), axis=0, keepdims=True)

    def tall(flat_row):
        spread = jnp.where(eye, jnp.broadcast_to(flat_row, (LANES, LANES)), 0.0)
        return jnp.broadcast_to(jnp.sum(spread, axis=1, keepdims=True), (LANES, LANES))

    def squares(block):
        wide = block.astype(jnp.float32)
        total = jnp.sum(wide * wide, axis=1, keepdims=True)
        return jnp.broadcast_to(total, (LANES, LANES))

    with jax.named_scope("column_norms"):

        def column_block(q, carry):
            span = pl.ds(pl.multiple_of(q * LANES, LANES), LANES)
            norm = squares(y_ref[span, :])
            v_wide[span, :] = -shift * norm
            cn[pl.ds(q, 1), :] = flat(norm)
            pair_wide[span, :] = pair_of(tile * n_col + q * LANES + line, col_ends)
            return carry

        lax.fori_loop(0, col_blocks, column_block, 0)

    row_box[0, tile] = jnp.zeros(row_box.shape[2:], jnp.float32)
    for h in range(2):
        row_box[0, tile, pl.ds(halves + h, 1), :] = flat(
            squares(rows[tile, pl.ds(h * half, half), :])
        )

    chunk = min(512, n_col)

    def score_block(block):
        first = group * (n_row * TILES) + block * n_row
        block_pair = [
            pair_of(first + h * half + lane[:1], row_ends) for h in range(2)
        ]

        def product(i, top):
            span = pl.ds(pl.multiple_of(i * chunk, chunk), chunk)
            cross = lax.dot_general(
                y_ref[span, :],
                rows[block],
                (((1,), (1,)), ((), ())),
                preferred_element_type=jnp.float32,
            )
            v = v_wide[span, :]
            col_pair = pair_wide[span, :]
            new = []
            for h in range(2):
                k = jnp.where(
                    col_pair == block_pair[h], cross[:, h * half : (h + 1) * half] * scale, NEG
                )
                scores[2 * block + h, span, :] = k
                new.append(
                    jnp.maximum(top[h], jnp.max((k + v).reshape(chunk // 8, 8, LANES), axis=0))
                )
            return tuple(new)

        start = jnp.full((8, LANES), 4 * NEG, jnp.float32)
        top = lax.fori_loop(0, n_col // chunk, product, (start, start))
        top = [jnp.max(t, axis=0, keepdims=True) for t in top]

        def total(i, so_far):
            span = pl.ds(pl.multiple_of(i * LANES, LANES), LANES)
            v = v_wide[span, :]
            new = []
            for h in range(2):
                e = jnp.exp2(scores[2 * block + h, span, :] + v - top[h])
                new.append(so_far[h] + jnp.sum(e.reshape(LANES // 8, 8, LANES), axis=0))
            return tuple(new)

        start = jnp.zeros((8, LANES), jnp.float32)
        sums = lax.fori_loop(0, n_col // LANES, total, (start, start))
        for h in range(2):
            row_box[0, tile, pl.ds(2 * block + h, 1), :] = top[h] + jnp.log2(
                jnp.sum(sums[h], axis=0, keepdims=True)
            )

    def score_blocks(dx, flip):
        score_block(at(dx, flip))

    with jax.named_scope("scores_near"):
        score_blocks(0, False)
        wait_half(SIB, 0)
        wait_half(SIB, 1)
        score_blocks(0, True)

    left_block, right_block = at(NX - 1, False), at(1, False)
    opposite = at(2, False)
    with jax.named_scope("forward"):
        wait_half(LEFT, 0)
        send_block(left_block, 0, right, OPP)
        send_block(left_block, 0, sib, LEFT_SIB)
        wait_half(RIGHT, 1)
        send_block(right_block, 1, left, OPP)
        send_block(right_block, 1, sib, RIGHT_SIB)
        wait_half(LEFT, 1)
        send_block(left_block, 1, sib, LEFT_SIB)
        wait_half(RIGHT, 0)
        send_block(right_block, 0, sib, RIGHT_SIB)

    with jax.named_scope("scores_sides"):

        def side(s, carry):
            score_block(2 * lax.rem(x + 1 + 2 * s, NX) + core)
            return carry

        lax.fori_loop(0, 2, side, 0)
        for part in range(2):
            wait_half(LEFT_SIB, part)
            wait_half(RIGHT_SIB, part)

        def other_side(s, carry):
            score_block(2 * lax.rem(x + 1 + 2 * s, NX) + 1 - core)
            return carry

        lax.fori_loop(0, 2, other_side, 0)

    with jax.named_scope("wait_opposite"):
        for part in range(2):
            wait_half(OPP, part)
            send_block(opposite, part, sib, OPP_SIB)
    with jax.named_scope("scores_opposite"):
        score_blocks(2, False)
        for part in range(2):
            wait_half(OPP_SIB, part)
        score_blocks(2, True)

    row_line = lax.broadcasted_iota(jnp.int32, (halves, LANES), 0)
    row_lane = lax.broadcasted_iota(jnp.int32, (halves, LANES), 1)
    row_pair = pair_of(group * (n_row * TILES) + row_line * half + row_lane, row_ends)
    log_cs = jnp.log2(size_of(row_pair, col_sizes))
    col_line = lax.broadcasted_iota(jnp.int32, (col_blocks, LANES), 0)
    col_lane = lax.broadcasted_iota(jnp.int32, (col_blocks, LANES), 1)
    col_pair = pair_of(tile * n_col + col_line * LANES + col_lane, col_ends)
    log_rs = jnp.log2(size_of(col_pair, row_sizes))

    def row_pass(step):
        def highest(i, top):
            span = pl.ds(pl.multiple_of(i * 8, 8), 8)
            return jnp.maximum(top, scores[:, span, :] + v_wide[span, :][None])

        start = jnp.full((halves, 8, LANES), 4 * NEG, jnp.float32)
        top = lax.fori_loop(0, n_col // 8, highest, start, unroll=4)
        top = jnp.max(top, axis=1)

        def total(i, so_far):
            span = pl.ds(pl.multiple_of(i * 8, 8), 8)
            return so_far + jnp.exp2(scores[:, span, :] + v_wide[span, :][None] - top[:, None, :])

        start = jnp.zeros((halves, 8, LANES), jnp.float32)
        sums = lax.fori_loop(0, n_col // 8, total, start, unroll=4)
        row_box[step, tile, :halves, :] = top + jnp.log2(jnp.sum(sums, axis=1))

    def column_pass(u):
        u_wide = jnp.broadcast_to(u[:, None, :], (halves, 8, LANES))

        def lanes(i, carry):
            span = pl.ds(pl.multiple_of(i * 8, 8), 8)
            t = scores[:, span, :] + u_wide
            top = jnp.max(t, axis=0)
            top_wide[span, :] = top
            sum_wide[span, :] = jnp.sum(jnp.exp2(t - top[None]), axis=0)
            return carry

        lax.fori_loop(0, n_col // 8, lanes, 0, unroll=2)

        def across(q, carry):
            span = pl.ds(pl.multiple_of(q * LANES, LANES), LANES)
            tops = top_wide[span, :]
            top = jnp.max(tops, axis=1, keepdims=True)
            total = jnp.sum(sum_wide[span, :] * jnp.exp2(tops - top), axis=1, keepdims=True)
            wide = (LANES, LANES)
            column[pl.ds(q, 1), :] = flat(jnp.broadcast_to(top, wide)) + jnp.log2(
                flat(jnp.broadcast_to(total, wide))
            )
            return carry

        lax.fori_loop(0, col_blocks, across, 0, unroll=2)
        return column[...]

    def share(box, step, me, size, targets, send, recv):
        own = box.at[step, len(targets) if me is None else me, pl.ds(0, size)]
        for i, to in enumerate(targets):
            pltpu.make_async_remote_copy(
                src_ref=own,
                dst_ref=box.at[step, i, pl.ds(0, size)] if me is None else own,
                send_sem=send,
                recv_sem=recv,
                device_id=to,
                device_id_type=MESH,
            ).start()
        some = box.at[step, pl.ds(0, len(targets)), pl.ds(0, size)]
        pltpu.make_async_copy(some, some, recv).wait()

    def sent(box, step, count, size, send):
        some = box.at[step, pl.ds(0, count), pl.ds(0, size)]
        pltpu.make_async_copy(some, some, send).wait()

    for step in range(ITERS):
        last = step + 1 == ITERS
        if step:
            with jax.named_scope("row_pass"):
                row_pass(step)
        with jax.named_scope("row_share"):
            share(
                row_box,
                step,
                tile,
                row_box.shape[2] if step == 0 else halves,
                [(group, lax.rem(tile + r, TILES)) for r in range(1, TILES)],
                send_sem.at[1 + step],
                row_sem.at[step],
            )
            u = log_cs - merged(row_box[step, :, :halves, :])
        with jax.named_scope("column_pass"):
            column_lse = column_pass(u)
        if not last:
            with jax.named_scope("column_share_near"):
                near_box[step, len(near)] = column_lse
                share(
                    near_box,
                    step,
                    None,
                    col_blocks,
                    near,
                    send_sem.at[1 + ITERS + step],
                    near_sem.at[step],
                )
                lse = merged(near_box[step])
                v = jnp.where(lse > EMPTY, log_rs - lse, 0.0)
        else:
            f = (EPS / LOG2E) * u
            f = f + jnp.concatenate(
                [row_box[0, t, halves : halves + 2, :] for t in range(TILES)], axis=0
            ) * (1.0 / depth)
            size = col_blocks + pair_count
            y_box[0, y, :col_blocks, :] = column_lse
            for k in range(pair_count):
                y_box[0, y, pl.ds(col_blocks + k, 1), :] = jnp.sum(
                    jnp.where(row_pair == k, f, 0.0), axis=0, keepdims=True
                )
            with jax.named_scope("column_share_y"):
                share(
                    y_box,
                    0,
                    y,
                    size,
                    [(in_y(r), tile) for r in range(1, NY)],
                    send_sem.at[2 * ITERS],
                    y_sem,
                )
                z_box[0, z, :col_blocks, :] = merged(y_box[0, :, :col_blocks, :])
                z_box[0, z, col_blocks:, :] = jnp.sum(y_box[0, :, col_blocks:, :], axis=0)
            with jax.named_scope("column_share_z"):
                share(
                    z_box,
                    0,
                    z,
                    size,
                    [(in_z(r), tile) for r in range(1, nz)],
                    send_sem.at[2 * ITERS + 1],
                    z_sem,
                )
                v = log_rs - merged(z_box[0, :, :col_blocks, :])
        if not last:
            with jax.named_scope("spread"):
                for q in range(col_blocks):
                    v_wide[pl.ds(q * LANES, LANES), :] = tall(v[q : q + 1, :])

    with jax.named_scope("results"):
        g_ref[...] = (EPS / LOG2E) * v + cn[...] * (1.0 / depth)
        sums = jnp.sum(z_box[0, :, col_blocks:, :], axis=0)
        sums = jnp.broadcast_to(jnp.sum(sums, axis=1, keepdims=True), (pair_count, LANES))
        value = jnp.zeros((2, LANES), jnp.float32)
        own_pair = jnp.zeros((2, LANES), jnp.int32)
        for t in range(TILES):
            value = jnp.where(tile == t, f[2 * t : 2 * t + 2], value)
            own_pair = jnp.where(tile == t, row_pair[2 * t : 2 * t + 2], own_pair)
        mean = jnp.zeros((2, LANES), jnp.float32)
        for k in range(pair_count):
            mean = jnp.where(own_pair == k, sums[k : k + 1, :], mean)
        f_ref[...] = value - mean / size_of(own_pair, row_sizes)

    with jax.named_scope("sent"):
        ref = rows.at[pl.ds(0, 7)]
        pltpu.make_async_copy(ref, ref, send_sem.at[0]).wait()
        for step in range(ITERS):
            width = row_box.shape[2] if step == 0 else halves
            sent(row_box, step, TILES - 1, width, send_sem.at[1 + step])
        for step in range(ITERS - 1):
            sent(near_box, step, len(near), col_blocks, send_sem.at[1 + ITERS + step])
        sent(y_box, 0, NY - 1, size, send_sem.at[2 * ITERS])
        sent(z_box, 0, nz - 1, size, send_sem.at[2 * ITERS + 1])


def local(candidates, validation, row_sizes, col_sizes):
    groups = lax.axis_size("pair")
    n_row, depth = candidates.shape
    n_col = validation.shape[0]
    pairs = row_sizes.shape[0]
    halves = 2 * TILES
    half = n_row // 2
    col_blocks = n_col // LANES
    vmem = pl.BlockSpec(memory_space=pltpu.VMEM)
    whole = pl.BlockSpec(memory_space=pl.ANY)
    near = 2 * -(-ROW_MOST // (n_row * TILES))
    row_value, col_potential = pl.pallas_call(
        functools.partial(kernel, pairs, groups),
        out_shape=(
            jax.ShapeDtypeStruct((2, half), jnp.float32),
            jax.ShapeDtypeStruct((col_blocks, LANES), jnp.float32),
        ),
        in_specs=[whole] * 4,
        out_specs=(vmem, vmem),
        scratch_shapes=[
            pltpu.SMEM((pairs,), jnp.int32),
            pltpu.SMEM((pairs,), jnp.int32),
            pltpu.VMEM((n_col, depth), jnp.bfloat16),
            pltpu.VMEM((TILES, n_row, depth), jnp.bfloat16),
            pltpu.VMEM((halves, n_col, half), jnp.float32),
            pltpu.VMEM((n_col, LANES), jnp.float32),
            pltpu.VMEM((n_col, LANES), jnp.int32),
            pltpu.VMEM((n_col, LANES), jnp.float32),
            pltpu.VMEM((n_col, LANES), jnp.float32),
            pltpu.VMEM((col_blocks, LANES), jnp.float32),
            pltpu.VMEM((col_blocks, LANES), jnp.float32),
            pltpu.VMEM((ITERS, TILES, halves + 8, half), jnp.float32),
            pltpu.VMEM((ITERS - 1, near + 1, col_blocks, LANES), jnp.float32),
            pltpu.VMEM((1, NY, col_blocks + pairs, LANES), jnp.float32),
            pltpu.VMEM((1, groups // NY, col_blocks + pairs, LANES), jnp.float32),
            pltpu.SemaphoreType.DMA((4,)),
            pltpu.SemaphoreType.DMA((2 * ITERS + 2,)),
            pltpu.SemaphoreType.DMA((7, 2)),
            pltpu.SemaphoreType.DMA((ITERS,)),
            pltpu.SemaphoreType.DMA((ITERS - 1,)),
            pltpu.SemaphoreType.DMA,
            pltpu.SemaphoreType.DMA,
        ],
        compiler_params=pltpu.CompilerParams(
            collective_id=0, has_side_effects=True, vmem_limit_bytes=56 * 2**20
        ),
    )(row_sizes, col_sizes, candidates, validation)
    return row_value.reshape(n_row), col_potential.reshape(n_col)


def solution(mesh):
    in_specs = (P(("pair", "tile"), None), P("tile", None), P(), P())
    out_specs = (P(("pair", "tile")), P("tile"))
    return jax.shard_map(local, mesh=mesh, in_specs=in_specs, out_specs=out_specs, check_vma=False)
```

```python
import functools
import math

import jax
import jax.numpy as jnp
from jax import lax
from jax.experimental import pallas as pl
from jax.experimental.pallas import tpu as pltpu
from jax.sharding import PartitionSpec as P

ITERS = 3
EPS = 0.02
NEG = -1e30
EMPTY = -1e29
TINY = 1e-37
LOG2E = math.log2(math.e)
NX, NY = 4, 4
TILES = 2 * NX
ROW_MOST = 24576
HOPS = 4
LANES = 128
MESH = pl.DeviceIdType.MESH


def pair_of(position, ends):
    pair = jnp.zeros(position.shape, jnp.int32)
    for end in ends:
        pair += (position >= end).astype(jnp.int32)
    return pair


def size_of(pair, sizes):
    size = jnp.zeros(pair.shape, jnp.float32)
    for k, s in enumerate(sizes):
        size = jnp.where(pair == k, s.astype(jnp.float32), size)
    return size


def merged(parts):
    top = jnp.max(parts, axis=0)
    return top + jnp.log2(jnp.sum(jnp.exp2(parts - top[None]), axis=0))


def kernel(
    pair_count,
    group_count,
    rs_hbm,
    cs_hbm,
    x_ref,
    y_hbm,
    f_ref,
    g_ref,
    rs_ref,
    cs_ref,
    y_ref,
    rows,
    scores,
    v_wide,
    pair_wide,
    top_wide,
    sum_wide,
    cn,
    column,
    row_box,
    near_box,
    y_box,
    z_box,
    local_sem,
    send_sem,
    block_sem,
    hop_sem,
    row_sem,
    near_sem,
    y_sem,
    z_sem,
):
    n_row, depth = x_ref.shape
    n_col = y_ref.shape[0]
    half = n_row // 2
    halves = 2 * TILES
    col_blocks = n_col // LANES
    nz = group_count // NY
    reach = -(-ROW_MOST // (n_row * TILES))
    scale = 2.0 * LOG2E / (depth * EPS)
    shift = LOG2E / (depth * EPS)

    group = lax.axis_index("pair")
    tile = lax.axis_index("tile")
    z, y = group // NY, lax.rem(group, NY)
    x, core = tile // 2, lax.rem(tile, 2)

    def at(dx, flip):
        other = 1 - core if flip else core
        return 2 * lax.rem(x + dx, NX) + other

    def in_y(r):
        return z * NY + lax.rem(y + r, NY)

    def in_z(r):
        return lax.rem(z + r, nz) * NY + y

    with jax.named_scope("greet"):
        near = [(lax.rem(group + r + group_count, group_count), tile) for r in range(-reach, reach + 1) if r]
        neighbours = [(in_y(1), tile), (in_y(NY - 1), tile), (in_z(1), tile), (in_z(nz - 1), tile)]
        copies = [
            pltpu.make_async_copy(a, b, local_sem.at[i])
            for i, (a, b) in enumerate(
                [(x_ref, rows.at[tile]), (rs_hbm, rs_ref), (cs_hbm, cs_ref), (y_hbm, y_ref)]
            )
        ]
        for copy in copies:
            copy.start()
        barrier = pltpu.get_barrier_semaphore()
        for to in neighbours + [(group, at(dx, flip)) for dx, flip in ((1, 0), (NX - 1, 0), (0, 1))]:
            pl.semaphore_signal(barrier, device_id=to, device_id_type=MESH)
        copies[0].wait()
        pl.semaphore_wait(barrier, len(neighbours) + 3)

    def tell(r):
        for to in neighbours:
            pl.semaphore_signal(hop_sem.at[r - 1], device_id=to, device_id_type=MESH)

    def told(r):
        pl.semaphore_wait(hop_sem.at[r - 1], len(neighbours))

    def send_block(block, part, to, sem, sent=0):
        ref = rows.at[block, pl.ds(part * half, half)]
        copy = pltpu.make_async_remote_copy(
            src_ref=ref,
            dst_ref=ref,
            send_sem=send_sem.at[sent],
            recv_sem=block_sem.at[sem, part],
            device_id=(group, to),
            device_id_type=MESH,
        )
        copy.start()

    def wait_half(sem, part):
        ref = rows.at[0, pl.ds(0, half)]
        pltpu.make_async_copy(ref, ref, block_sem.at[sem, part]).wait()

    SIB, LEFT, RIGHT, LEFT_SIB, RIGHT_SIB, OPP, OPP_SIB = range(7)
    right, left, sib = at(1, False), at(NX - 1, False), at(0, True)

    with jax.named_scope("send_own"):
        send_block(tile, 0, right, LEFT, 1)
        send_block(tile, 1, left, RIGHT, 1)
        send_block(tile, 0, sib, SIB)
        send_block(tile, 1, sib, SIB)
        tell(1)

    with jax.named_scope("inputs"):
        for copy in copies[1:]:
            copy.wait()

    row_ends, col_ends = [], []
    row_sizes, col_sizes = [], []
    for k in range(pair_count):
        row_sizes.append(rs_ref[k])
        col_sizes.append(cs_ref[k])
        row_ends.append(row_sizes[k] + (row_ends[-1] if k else 0))
        col_ends.append(col_sizes[k] + (col_ends[-1] if k else 0))

    lane = lax.broadcasted_iota(jnp.int32, (LANES, LANES), 1)
    line = lax.broadcasted_iota(jnp.int32, (LANES, LANES), 0)
    eye = lane == line

    def flat(tall):
        return jnp.sum(jnp.where(eye, tall, 0.0), axis=0, keepdims=True)

    def tall(flat_row):
        spread = jnp.where(eye, jnp.broadcast_to(flat_row, (LANES, LANES)), 0.0)
        return jnp.broadcast_to(jnp.sum(spread, axis=1, keepdims=True), (LANES, LANES))

    def squares(block):
        wide = block.astype(jnp.float32)
        total = jnp.sum(wide * wide, axis=1, keepdims=True)
        return jnp.broadcast_to(total, (LANES, LANES))

    with jax.named_scope("column_norms"):

        def column_block(q, carry):
            span = pl.ds(pl.multiple_of(q * LANES, LANES), LANES)
            norm = squares(y_ref[span, :])
            v_wide[span, :] = -shift * norm
            cn[pl.ds(q, 1), :] = flat(norm)
            pair_wide[span, :] = pair_of(tile * n_col + q * LANES + line, col_ends)
            return carry

        lax.fori_loop(0, col_blocks, column_block, 0)

    row_box[0, tile] = jnp.zeros(row_box.shape[2:], jnp.float32)
    for h in range(2):
        row_box[0, tile, pl.ds(halves + h, 1), :] = flat(
            squares(rows[tile, pl.ds(h * half, half), :])
        )

    chunk = min(512, n_col)

    def score_block(block):
        first = group * (n_row * TILES) + block * n_row
        block_pair = [
            pair_of(first + h * half + lane[:1], row_ends) for h in range(2)
        ]

        def product(i, top):
            span = pl.ds(pl.multiple_of(i * chunk, chunk), chunk)
            cross = lax.dot_general(
                y_ref[span, :],
                rows[block],
                (((1,), (1,)), ((), ())),
                preferred_element_type=jnp.float32,
            )
            v = v_wide[span, :]
            col_pair = pair_wide[span, :]
            new = []
            for h in range(2):
                k = jnp.where(
                    col_pair == block_pair[h], cross[:, h * half : (h + 1) * half] * scale, NEG
                )
                scores[2 * block + h, span, :] = k
                new.append(
                    jnp.maximum(top[h], jnp.max((k + v).reshape(chunk // 8, 8, LANES), axis=0))
                )
            return tuple(new)

        start = jnp.full((8, LANES), 4 * NEG, jnp.float32)
        top = lax.fori_loop(0, n_col // chunk, product, (start, start))
        top = [jnp.max(t, axis=0, keepdims=True) for t in top]

        def total(i, so_far):
            span = pl.ds(pl.multiple_of(i * LANES, LANES), LANES)
            v = v_wide[span, :]
            new = []
            for h in range(2):
                e = jnp.exp2(scores[2 * block + h, span, :] + v - top[h])
                new.append(so_far[h] + jnp.sum(e.reshape(LANES // 8, 8, LANES), axis=0))
            return tuple(new)

        start = jnp.zeros((8, LANES), jnp.float32)
        sums = lax.fori_loop(0, n_col // LANES, total, (start, start))
        for h in range(2):
            row_box[0, tile, pl.ds(2 * block + h, 1), :] = top[h] + jnp.log2(
                jnp.sum(sums[h], axis=0, keepdims=True)
            )

    def score_blocks(dx, flip):
        score_block(at(dx, flip))

    with jax.named_scope("scores_near"):
        score_blocks(0, False)
        wait_half(SIB, 0)
        wait_half(SIB, 1)
        score_blocks(0, True)

    with jax.named_scope("send_own_rest"):
        pltpu.make_async_copy(rows.at[0], rows.at[0], send_sem.at[1]).wait()
        send_block(tile, 1, right, LEFT)
        send_block(tile, 0, left, RIGHT)
        told(1)
        tell(2)

    left_block, right_block = at(NX - 1, False), at(1, False)
    opposite = at(2, False)
    with jax.named_scope("forward"):
        wait_half(LEFT, 0)
        send_block(left_block, 0, right, OPP)
        send_block(left_block, 0, sib, LEFT_SIB)
        wait_half(RIGHT, 1)
        send_block(right_block, 1, left, OPP)
        send_block(right_block, 1, sib, RIGHT_SIB)
        wait_half(LEFT, 1)
        send_block(left_block, 1, sib, LEFT_SIB)
        wait_half(RIGHT, 0)
        send_block(right_block, 0, sib, RIGHT_SIB)
        told(2)
        tell(3)

    with jax.named_scope("scores_sides"):

        def side(s, carry):
            score_block(2 * lax.rem(x + 1 + 2 * s, NX) + core)
            return carry

        lax.fori_loop(0, 2, side, 0)
        for part in range(2):
            wait_half(LEFT_SIB, part)
            wait_half(RIGHT_SIB, part)

        def other_side(s, carry):
            score_block(2 * lax.rem(x + 1 + 2 * s, NX) + 1 - core)
            return carry

        lax.fori_loop(0, 2, other_side, 0)
        told(3)
        tell(4)

    with jax.named_scope("wait_opposite"):
        for part in range(2):
            wait_half(OPP, part)
            send_block(opposite, part, sib, OPP_SIB)
    with jax.named_scope("scores_opposite"):
        score_blocks(2, False)
        for part in range(2):
            wait_half(OPP_SIB, part)
        score_blocks(2, True)

    row_line = lax.broadcasted_iota(jnp.int32, (halves, LANES), 0)
    row_lane = lax.broadcasted_iota(jnp.int32, (halves, LANES), 1)
    row_pair = pair_of(group * (n_row * TILES) + row_line * half + row_lane, row_ends)
    cs_of_row = size_of(row_pair, col_sizes)
    log_cs = jnp.log2(cs_of_row)
    col_line = lax.broadcasted_iota(jnp.int32, (col_blocks, LANES), 0)
    col_lane = lax.broadcasted_iota(jnp.int32, (col_blocks, LANES), 1)
    col_pair = pair_of(tile * n_col + col_line * LANES + col_lane, col_ends)
    rs_of_col = size_of(col_pair, row_sizes)
    log_rs = jnp.log2(rs_of_col)

    def row_sums():
        def add(i, so_far):
            span = pl.ds(pl.multiple_of(i * 8, 8), 8)
            return so_far + scores[:, span, :] * v_wide[span, :][None]

        start = jnp.zeros((halves, 8, LANES), jnp.float32)
        return jnp.sum(lax.fori_loop(0, n_col // 8, add, start, unroll=4), axis=1)

    def first_column_pass(u):
        u_wide = jnp.broadcast_to(u[:, None, :], (halves, 8, LANES))

        def lanes(i, carry):
            span = pl.ds(pl.multiple_of(i * 8, 8), 8)
            t = scores[:, span, :] + u_wide
            top = jnp.max(t, axis=0)
            e = jnp.exp2(t - top[None])
            scores[:, span, :] = e
            top_wide[span, :] = top
            sum_wide[span, :] = jnp.sum(e, axis=0)
            return carry

        lax.fori_loop(0, n_col // 8, lanes, 0, unroll=4)

        def across(q, carry):
            span = pl.ds(pl.multiple_of(q * LANES, LANES), LANES)
            tops = top_wide[span, :]
            top = jnp.max(tops, axis=1, keepdims=True)
            total = jnp.sum(sum_wide[span, :] * jnp.exp2(tops - top), axis=1, keepdims=True)
            wide = (LANES, LANES)
            column[pl.ds(q, 1), :] = flat(jnp.broadcast_to(top, wide)) + jnp.log2(
                flat(jnp.broadcast_to(total, wide))
            )
            return carry

        lax.fori_loop(0, col_blocks, across, 0, unroll=2)
        return column[...]

    def column_sums(b):
        b_wide = jnp.broadcast_to(b[:, None, :], (halves, 8, LANES))

        def lanes(i, carry):
            span = pl.ds(pl.multiple_of(i * 8, 8), 8)
            sum_wide[span, :] = jnp.sum(scores[:, span, :] * b_wide, axis=0) * top_wide[span, :]
            return carry

        lax.fori_loop(0, n_col // 8, lanes, 0, unroll=4)

        def across(q, carry):
            span = pl.ds(pl.multiple_of(q * LANES, LANES), LANES)
            total = jnp.sum(sum_wide[span, :], axis=1, keepdims=True)
            column[pl.ds(q, 1), :] = flat(jnp.broadcast_to(total, (LANES, LANES)))
            return carry

        lax.fori_loop(0, col_blocks, across, 0, unroll=2)
        return column[...]

    def share(box, step, me, size, targets, send, recv):
        own = box.at[step, len(targets) if me is None else me, pl.ds(0, size)]
        for i, to in enumerate(targets):
            pltpu.make_async_remote_copy(
                src_ref=own,
                dst_ref=box.at[step, i, pl.ds(0, size)] if me is None else own,
                send_sem=send,
                recv_sem=recv,
                device_id=to,
                device_id_type=MESH,
            ).start()
        some = box.at[step, pl.ds(0, len(targets)), pl.ds(0, size)]
        pltpu.make_async_copy(some, some, recv).wait()

    def sent(box, step, count, size, send):
        some = box.at[step, pl.ds(0, count), pl.ds(0, size)]
        pltpu.make_async_copy(some, some, send).wait()

    def share_rows(step):
        share(
            row_box,
            step,
            tile,
            row_box.shape[2] if step == 0 else halves,
            [(group, lax.rem(tile + r, TILES)) for r in range(1, TILES)],
            send_sem.at[2 + step],
            row_sem.at[step],
        )
        return row_box[step, :, :halves, :]

    def share_columns(step, own):
        near_box[step, len(near)] = own
        share(
            near_box,
            step,
            None,
            col_blocks,
            near,
            send_sem.at[2 + ITERS + step],
            near_sem.at[step],
        )
        return near_box[step]

    with jax.named_scope("row_share"):
        u = log_cs - merged(share_rows(0))
    with jax.named_scope("column_pass"):
        column_lse = first_column_pass(u)
    told(HOPS)
    with jax.named_scope("column_share"):
        lse = merged(share_columns(0, column_lse))
        v = jnp.where(lse > EMPTY, log_rs - lse, 0.0)

    row_factor = jnp.ones((halves, LANES), jnp.float32)
    with jax.named_scope("spread"):
        for q in range(col_blocks):
            span = pl.ds(q * LANES, LANES)
            wide = jnp.exp2(top_wide[span, :] + tall(v[q : q + 1, :]))
            top_wide[span, :] = wide
            v_wide[span, :] = wide
    for step in range(1, ITERS):
        last = step + 1 == ITERS
        with jax.named_scope("row_pass"):
            row_box[step, tile, :halves, :] = row_sums()
        with jax.named_scope("row_share"):
            row_factor = cs_of_row / jnp.sum(share_rows(step), axis=0)
        with jax.named_scope("column_pass"):
            own = column_sums(row_factor)
        if not last:
            with jax.named_scope("column_share"):
                total = jnp.sum(share_columns(step, own), axis=0)
                factor = rs_of_col / jnp.maximum(total, 2.0**-60)
            with jax.named_scope("spread"):
                for q in range(col_blocks):
                    span = pl.ds(q * LANES, LANES)
                    v_wide[span, :] = top_wide[span, :] * tall(factor[q : q + 1, :])
    f = (EPS / LOG2E) * (u + jnp.log2(row_factor))
    f = f + jnp.concatenate(
        [row_box[0, t, halves : halves + 2, :] for t in range(TILES)], axis=0
    ) * (1.0 / depth)
    size = col_blocks + pair_count
    y_box[0, y, :col_blocks, :] = jnp.where(
        own > 0.0, jnp.log2(jnp.maximum(own, TINY)) - v, NEG
    )
    for k in range(pair_count):
        y_box[0, y, pl.ds(col_blocks + k, 1), :] = jnp.sum(
            jnp.where(row_pair == k, f, 0.0), axis=0, keepdims=True
        )
    with jax.named_scope("column_share_y"):
        share(
            y_box,
            0,
            y,
            size,
            [(in_y(r), tile) for r in range(1, NY)],
            send_sem.at[1 + 2 * ITERS],
            y_sem,
        )
        z_box[0, z, :col_blocks, :] = merged(y_box[0, :, :col_blocks, :])
        z_box[0, z, col_blocks:, :] = jnp.sum(y_box[0, :, col_blocks:, :], axis=0)
    with jax.named_scope("column_share_z"):
        share(
            z_box,
            0,
            z,
            size,
            [(in_z(r), tile) for r in range(1, nz)],
            send_sem.at[2 + 2 * ITERS],
            z_sem,
        )
        v = log_rs - merged(z_box[0, :, :col_blocks, :])

    with jax.named_scope("results"):
        g_ref[...] = (EPS / LOG2E) * v + cn[...] * (1.0 / depth)
        sums = jnp.sum(z_box[0, :, col_blocks:, :], axis=0)
        sums = jnp.broadcast_to(jnp.sum(sums, axis=1, keepdims=True), (pair_count, LANES))
        value = jnp.zeros((2, LANES), jnp.float32)
        own_pair = jnp.zeros((2, LANES), jnp.int32)
        for t in range(TILES):
            value = jnp.where(tile == t, f[2 * t : 2 * t + 2], value)
            own_pair = jnp.where(tile == t, row_pair[2 * t : 2 * t + 2], own_pair)
        mean = jnp.zeros((2, LANES), jnp.float32)
        for k in range(pair_count):
            mean = jnp.where(own_pair == k, sums[k : k + 1, :], mean)
        f_ref[...] = value - mean / size_of(own_pair, row_sizes)

    with jax.named_scope("sent"):
        ref = rows.at[pl.ds(0, 6)]
        pltpu.make_async_copy(ref, ref, send_sem.at[0]).wait()
        for step in range(ITERS):
            width = row_box.shape[2] if step == 0 else halves
            sent(row_box, step, TILES - 1, width, send_sem.at[2 + step])
        for step in range(ITERS - 1):
            sent(near_box, step, len(near), col_blocks, send_sem.at[2 + ITERS + step])
        sent(y_box, 0, NY - 1, size, send_sem.at[1 + 2 * ITERS])
        sent(z_box, 0, nz - 1, size, send_sem.at[2 + 2 * ITERS])


def local(candidates, validation, row_sizes, col_sizes):
    groups = lax.axis_size("pair")
    n_row, depth = candidates.shape
    n_col = validation.shape[0]
    pairs = row_sizes.shape[0]
    halves = 2 * TILES
    half = n_row // 2
    col_blocks = n_col // LANES
    vmem = pl.BlockSpec(memory_space=pltpu.VMEM)
    whole = pl.BlockSpec(memory_space=pl.ANY)
    near = 2 * -(-ROW_MOST // (n_row * TILES))
    row_value, col_potential = pl.pallas_call(
        functools.partial(kernel, pairs, groups),
        out_shape=(
            jax.ShapeDtypeStruct((2, half), jnp.float32),
            jax.ShapeDtypeStruct((col_blocks, LANES), jnp.float32),
        ),
        in_specs=[whole] * 4,
        out_specs=(vmem, vmem),
        scratch_shapes=[
            pltpu.SMEM((pairs,), jnp.int32),
            pltpu.SMEM((pairs,), jnp.int32),
            pltpu.VMEM((n_col, depth), jnp.bfloat16),
            pltpu.VMEM((TILES, n_row, depth), jnp.bfloat16),
            pltpu.VMEM((halves, n_col, half), jnp.float32),
            pltpu.VMEM((n_col, LANES), jnp.float32),
            pltpu.VMEM((n_col, LANES), jnp.int32),
            pltpu.VMEM((n_col, LANES), jnp.float32),
            pltpu.VMEM((n_col, LANES), jnp.float32),
            pltpu.VMEM((col_blocks, LANES), jnp.float32),
            pltpu.VMEM((col_blocks, LANES), jnp.float32),
            pltpu.VMEM((ITERS, TILES, halves + 8, half), jnp.float32),
            pltpu.VMEM((ITERS - 1, near + 1, col_blocks, LANES), jnp.float32),
            pltpu.VMEM((1, NY, col_blocks + pairs, LANES), jnp.float32),
            pltpu.VMEM((1, groups // NY, col_blocks + pairs, LANES), jnp.float32),
            pltpu.SemaphoreType.DMA((4,)),
            pltpu.SemaphoreType.DMA((2 * ITERS + 3,)),
            pltpu.SemaphoreType.DMA((7, 2)),
            pltpu.SemaphoreType.REGULAR((HOPS,)),
            pltpu.SemaphoreType.DMA((ITERS,)),
            pltpu.SemaphoreType.DMA((ITERS - 1,)),
            pltpu.SemaphoreType.DMA,
            pltpu.SemaphoreType.DMA,
        ],
        compiler_params=pltpu.CompilerParams(
            collective_id=0, has_side_effects=True, vmem_limit_bytes=56 * 2**20
        ),
    )(row_sizes, col_sizes, candidates, validation)
    return row_value.reshape(n_row), col_potential.reshape(n_col)


def solution(mesh):
    in_specs = (P(("pair", "tile"), None), P("tile", None), P(), P())
    out_specs = (P(("pair", "tile")), P("tile"))
    return jax.shard_map(local, mesh=mesh, in_specs=in_specs, out_specs=out_specs, check_vma=False)
```

```python
import functools
import math

import jax
import jax.numpy as jnp
from jax import lax
from jax.experimental import pallas as pl
from jax.experimental.pallas import tpu as pltpu
from jax.sharding import PartitionSpec as P

ITERS = 3
EPS = 0.02
NEG = -1e30
EMPTY = -1e29
TINY = 1e-37
LOG2E = math.log2(math.e)
NX, NY = 4, 4
TILES = 2 * NX
ROW_MOST = 24576
HOPS = 4
TILE_ORDER = ((2, 0), (2, 1), (1, 1), (3, 1), (1, 0), (3, 0), (0, 1))
LANES = 128
MESH = pl.DeviceIdType.MESH


def pair_of(position, ends):
    pair = jnp.zeros(position.shape, jnp.int32)
    for end in ends:
        pair += (position >= end).astype(jnp.int32)
    return pair


def size_of(pair, sizes):
    size = jnp.zeros(pair.shape, jnp.float32)
    for k, s in enumerate(sizes):
        size = jnp.where(pair == k, s.astype(jnp.float32), size)
    return size


def merged(parts):
    top = jnp.max(parts, axis=0)
    return top + jnp.log2(jnp.sum(jnp.exp2(parts - top[None]), axis=0))


def kernel(
    pair_count,
    group_count,
    rs_hbm,
    cs_hbm,
    x_ref,
    y_hbm,
    f_ref,
    g_ref,
    rs_ref,
    cs_ref,
    y_ref,
    rows,
    scores,
    v_wide,
    pair_wide,
    top_wide,
    sum_wide,
    cn,
    column,
    row_box,
    near_box,
    y_box,
    z_box,
    local_sem,
    send_sem,
    block_sem,
    hop_sem,
    row_sem,
    near_sem,
    y_sem,
    z_sem,
):
    n_row, depth = x_ref.shape
    n_col = y_ref.shape[0]
    half = n_row // 2
    halves = 2 * TILES
    col_blocks = n_col // LANES
    nz = group_count // NY
    reach = -(-ROW_MOST // (n_row * TILES))
    scale = 2.0 * LOG2E / (depth * EPS)
    shift = LOG2E / (depth * EPS)

    group = lax.axis_index("pair")
    tile = lax.axis_index("tile")
    z, y = group // NY, lax.rem(group, NY)
    x, core = tile // 2, lax.rem(tile, 2)

    def at(dx, flip):
        other = 1 - core if flip else core
        return 2 * lax.rem(x + dx, NX) + other

    def in_y(r):
        return z * NY + lax.rem(y + r, NY)

    def in_z(r):
        return lax.rem(z + r, nz) * NY + y

    with jax.named_scope("greet"):
        offsets = sorted((r for r in range(-reach, reach + 1) if r), key=lambda r: -abs(r))
        near = [(lax.rem(group + r + group_count, group_count), tile) for r in offsets]
        neighbours = [(in_y(1), tile), (in_y(NY - 1), tile), (in_z(1), tile), (in_z(nz - 1), tile)]
        copies = [
            pltpu.make_async_copy(a, b, local_sem.at[i])
            for i, (a, b) in enumerate(
                [(x_ref, rows.at[tile]), (rs_hbm, rs_ref), (cs_hbm, cs_ref), (y_hbm, y_ref)]
            )
        ]
        for copy in copies:
            copy.start()
        barrier = pltpu.get_barrier_semaphore()
        for to in neighbours + [(group, at(dx, flip)) for dx, flip in ((1, 0), (NX - 1, 0), (0, 1))]:
            pl.semaphore_signal(barrier, device_id=to, device_id_type=MESH)
        copies[0].wait()
        pl.semaphore_wait(barrier, len(neighbours) + 3)

    def tell(r):
        for to in neighbours:
            pl.semaphore_signal(hop_sem.at[r - 1], device_id=to, device_id_type=MESH)

    def told(r):
        pl.semaphore_wait(hop_sem.at[r - 1], len(neighbours))

    def send_block(block, part, to, sem):
        ref = rows.at[block, pl.ds(part * half, half)]
        copy = pltpu.make_async_remote_copy(
            src_ref=ref,
            dst_ref=ref,
            send_sem=send_sem.at[0],
            recv_sem=block_sem.at[sem, part],
            device_id=(group, to),
            device_id_type=MESH,
        )
        copy.start()

    def wait_half(sem, part):
        ref = rows.at[0, pl.ds(0, half)]
        pltpu.make_async_copy(ref, ref, block_sem.at[sem, part]).wait()

    SIB, LEFT, RIGHT, LEFT_SIB, RIGHT_SIB, OPP, OPP_SIB = range(7)
    right, left, sib = at(1, False), at(NX - 1, False), at(0, True)

    with jax.named_scope("send_own"):
        send_block(tile, 0, right, LEFT)
        send_block(tile, 1, left, RIGHT)
        send_block(tile, 0, sib, SIB)
        send_block(tile, 1, sib, SIB)
        tell(1)

    with jax.named_scope("inputs"):
        for copy in copies[1:]:
            copy.wait()

    row_ends, col_ends = [], []
    row_sizes, col_sizes = [], []
    for k in range(pair_count):
        row_sizes.append(rs_ref[k])
        col_sizes.append(cs_ref[k])
        row_ends.append(row_sizes[k] + (row_ends[-1] if k else 0))
        col_ends.append(col_sizes[k] + (col_ends[-1] if k else 0))

    lane = lax.broadcasted_iota(jnp.int32, (LANES, LANES), 1)
    line = lax.broadcasted_iota(jnp.int32, (LANES, LANES), 0)
    eye = lane == line

    def flat(tall):
        return jnp.sum(jnp.where(eye, tall, 0.0), axis=0, keepdims=True)

    def tall(flat_row):
        spread = jnp.where(eye, jnp.broadcast_to(flat_row, (LANES, LANES)), 0.0)
        return jnp.broadcast_to(jnp.sum(spread, axis=1, keepdims=True), (LANES, LANES))

    def squares(block):
        wide = block.astype(jnp.float32)
        total = jnp.sum(wide * wide, axis=1, keepdims=True)
        return jnp.broadcast_to(total, (LANES, LANES))

    with jax.named_scope("column_norms"):

        def column_block(q, carry):
            span = pl.ds(pl.multiple_of(q * LANES, LANES), LANES)
            norm = squares(y_ref[span, :])
            v_wide[span, :] = -shift * norm
            cn[pl.ds(q, 1), :] = flat(norm)
            pair_wide[span, :] = pair_of(tile * n_col + q * LANES + line, col_ends)
            return carry

        lax.fori_loop(0, col_blocks, column_block, 0)

    row_box[0, tile] = jnp.zeros(row_box.shape[2:], jnp.float32)
    for h in range(2):
        row_box[0, tile, pl.ds(halves + h, 1), :] = flat(
            squares(rows[tile, pl.ds(h * half, half), :])
        )

    chunk = min(512, n_col)

    def score_block(block):
        first = group * (n_row * TILES) + block * n_row
        block_pair = [
            pair_of(first + h * half + lane[:1], row_ends) for h in range(2)
        ]

        def product(i, top):
            span = pl.ds(pl.multiple_of(i * chunk, chunk), chunk)
            cross = lax.dot_general(
                y_ref[span, :],
                rows[block],
                (((1,), (1,)), ((), ())),
                preferred_element_type=jnp.float32,
            )
            v = v_wide[span, :].reshape(chunk // 8, 8, LANES)
            col_pair = pair_wide[span, :]
            new = []
            for h in range(2):
                k = jnp.where(
                    col_pair == block_pair[h], cross[:, h * half : (h + 1) * half] * scale, NEG
                )
                k = k.reshape(chunk // 8, 8, LANES)
                scores[pl.ds(i * (chunk // 8), chunk // 8), 2 * block + h] = k
                new.append(jnp.maximum(top[h], jnp.max(k + v, axis=0)))
            return tuple(new)

        start = jnp.full((8, LANES), 4 * NEG, jnp.float32)
        top = lax.fori_loop(0, n_col // chunk, product, (start, start))
        top = [jnp.max(t, axis=0, keepdims=True) for t in top]

        def total(i, so_far):
            span = pl.ds(pl.multiple_of(i * LANES, LANES), LANES)
            v = v_wide[span, :].reshape(LANES // 8, 8, LANES)
            new = []
            for h in range(2):
                k = scores[pl.ds(i * (LANES // 8), LANES // 8), 2 * block + h]
                new.append(so_far[h] + jnp.sum(jnp.exp2(k + v - top[h][None]), axis=0))
            return tuple(new)

        start = jnp.zeros((8, LANES), jnp.float32)
        sums = lax.fori_loop(0, n_col // LANES, total, (start, start))
        for h in range(2):
            row_box[0, tile, pl.ds(2 * block + h, 1), :] = top[h] + jnp.log2(
                jnp.sum(sums[h], axis=0, keepdims=True)
            )

    def score_blocks(dx, flip):
        score_block(at(dx, flip))

    with jax.named_scope("scores_near"):
        score_blocks(0, False)
        send_block(tile, 1, right, LEFT)
        send_block(tile, 0, left, RIGHT)
        wait_half(SIB, 0)
        wait_half(SIB, 1)
        score_blocks(0, True)
        told(1)
        tell(2)

    left_block, right_block = at(NX - 1, False), at(1, False)
    opposite = at(2, False)
    with jax.named_scope("forward"):
        wait_half(LEFT, 0)
        send_block(left_block, 0, right, OPP)
        send_block(left_block, 0, sib, LEFT_SIB)
        wait_half(RIGHT, 1)
        send_block(right_block, 1, left, OPP)
        send_block(right_block, 1, sib, RIGHT_SIB)
        wait_half(LEFT, 1)
        send_block(left_block, 1, sib, LEFT_SIB)
        wait_half(RIGHT, 0)
        send_block(right_block, 0, sib, RIGHT_SIB)
        told(2)
        tell(3)

    with jax.named_scope("scores_sides"):

        def side(s, carry):
            score_block(2 * lax.rem(x + 1 + 2 * s, NX) + core)
            return carry

        lax.fori_loop(0, 2, side, 0)
        for part in range(2):
            wait_half(LEFT_SIB, part)
            wait_half(RIGHT_SIB, part)

        def other_side(s, carry):
            score_block(2 * lax.rem(x + 1 + 2 * s, NX) + 1 - core)
            return carry

        lax.fori_loop(0, 2, other_side, 0)
        told(3)
        tell(4)

    with jax.named_scope("wait_opposite"):
        for part in range(2):
            wait_half(OPP, part)
            send_block(opposite, part, sib, OPP_SIB)
    with jax.named_scope("scores_opposite"):
        score_blocks(2, False)
        for part in range(2):
            wait_half(OPP_SIB, part)
        score_blocks(2, True)

    row_line = lax.broadcasted_iota(jnp.int32, (halves, LANES), 0)
    row_lane = lax.broadcasted_iota(jnp.int32, (halves, LANES), 1)
    row_pair = pair_of(group * (n_row * TILES) + row_line * half + row_lane, row_ends)
    cs_of_row = size_of(row_pair, col_sizes)
    log_cs = jnp.log2(cs_of_row)
    col_line = lax.broadcasted_iota(jnp.int32, (col_blocks, LANES), 0)
    col_lane = lax.broadcasted_iota(jnp.int32, (col_blocks, LANES), 1)
    col_pair = pair_of(tile * n_col + col_line * LANES + col_lane, col_ends)
    rs_of_col = size_of(col_pair, row_sizes)
    log_rs = jnp.log2(rs_of_col)

    def row_sums():
        def add(i, so_far):
            span = pl.ds(pl.multiple_of(i * 8, 8), 8)
            return so_far + scores[i] * v_wide[span, :][None]

        start = jnp.zeros((halves, 8, LANES), jnp.float32)
        return jnp.sum(lax.fori_loop(0, n_col // 8, add, start, unroll=4), axis=1)

    def first_column_pass(u):
        u_wide = jnp.broadcast_to(u[:, None, :], (halves, 8, LANES))

        def lanes(i, carry):
            span = pl.ds(pl.multiple_of(i * 8, 8), 8)
            t = scores[i] + u_wide
            top = jnp.max(t, axis=0)
            e = jnp.exp2(t - top[None])
            scores[i] = e
            top_wide[span, :] = top
            sum_wide[span, :] = jnp.sum(e, axis=0)
            return carry

        lax.fori_loop(0, n_col // 8, lanes, 0, unroll=4)

        def across(q, carry):
            span = pl.ds(pl.multiple_of(q * LANES, LANES), LANES)
            tops = top_wide[span, :]
            top = jnp.max(tops, axis=1, keepdims=True)
            total = jnp.sum(sum_wide[span, :] * jnp.exp2(tops - top), axis=1, keepdims=True)
            wide = (LANES, LANES)
            column[pl.ds(q, 1), :] = flat(jnp.broadcast_to(top, wide)) + jnp.log2(
                flat(jnp.broadcast_to(total, wide))
            )
            return carry

        lax.fori_loop(0, col_blocks, across, 0, unroll=2)
        return column[...]

    def column_sums(b):
        b_wide = jnp.broadcast_to(b[:, None, :], (halves, 8, LANES))
        groups = LANES // 8

        def some(q, carry):
            flat_sum = jnp.zeros((8, LANES), jnp.float32)
            for j in range(groups):
                i = q * groups + j
                span = pl.ds(pl.multiple_of(i * 8, 8), 8)
                lanes = jnp.sum(scores[i] * b_wide, axis=0) * top_wide[span, :]
                total = jnp.broadcast_to(jnp.sum(lanes, axis=1, keepdims=True), (8, LANES))
                flat_sum = jnp.where(eye[8 * j : 8 * j + 8], total, flat_sum)
            column[pl.ds(q, 1), :] = jnp.sum(flat_sum, axis=0, keepdims=True)
            return carry

        lax.fori_loop(0, col_blocks, some, 0)
        return column[...]

    def share(box, step, me, size, targets, send, recv):
        own = box.at[step, len(targets) if me is None else me, pl.ds(0, size)]
        for i, to in enumerate(targets):
            pltpu.make_async_remote_copy(
                src_ref=own,
                dst_ref=box.at[step, i, pl.ds(0, size)] if me is None else own,
                send_sem=send,
                recv_sem=recv,
                device_id=to,
                device_id_type=MESH,
            ).start()
        some = box.at[step, pl.ds(0, len(targets)), pl.ds(0, size)]
        pltpu.make_async_copy(some, some, recv).wait()

    def sent(box, step, count, size, send):
        some = box.at[step, pl.ds(0, count), pl.ds(0, size)]
        pltpu.make_async_copy(some, some, send).wait()

    def share_rows(step):
        share(
            row_box,
            step,
            tile,
            row_box.shape[2] if step == 0 else halves,
            [(group, at(dx, flip)) for dx, flip in TILE_ORDER],
            send_sem.at[2 + step],
            row_sem.at[step],
        )
        return row_box[step, :, :halves, :]

    def share_columns(step, own):
        near_box[step, len(near)] = own
        share(
            near_box,
            step,
            None,
            col_blocks,
            near,
            send_sem.at[2 + ITERS + step],
            near_sem.at[step],
        )
        return near_box[step]

    with jax.named_scope("row_share"):
        u = log_cs - merged(share_rows(0))
    with jax.named_scope("column_pass"):
        column_lse = first_column_pass(u)
    told(HOPS)
    with jax.named_scope("column_share"):
        lse = merged(share_columns(0, column_lse))
        v = jnp.where(lse > EMPTY, log_rs - lse, 0.0)

    row_factor = jnp.ones((halves, LANES), jnp.float32)
    with jax.named_scope("spread"):
        for q in range(col_blocks):
            span = pl.ds(q * LANES, LANES)
            wide = jnp.exp2(top_wide[span, :] + tall(v[q : q + 1, :]))
            top_wide[span, :] = wide
            v_wide[span, :] = wide
    for step in range(1, ITERS):
        last = step + 1 == ITERS
        with jax.named_scope("row_pass"):
            row_box[step, tile, :halves, :] = row_sums()
        with jax.named_scope("row_share"):
            row_factor = cs_of_row / jnp.sum(share_rows(step), axis=0)
        with jax.named_scope("column_pass"):
            own = column_sums(row_factor)
        if not last:
            with jax.named_scope("column_share"):
                total = jnp.sum(share_columns(step, own), axis=0)
                factor = rs_of_col / jnp.maximum(total, 2.0**-60)
            with jax.named_scope("spread"):
                for q in range(col_blocks):
                    span = pl.ds(q * LANES, LANES)
                    v_wide[span, :] = top_wide[span, :] * tall(factor[q : q + 1, :])
    f = (EPS / LOG2E) * (u + jnp.log2(row_factor))
    f = f + jnp.concatenate(
        [row_box[0, t, halves : halves + 2, :] for t in range(TILES)], axis=0
    ) * (1.0 / depth)
    size = col_blocks + 1
    y_box[0, y, :col_blocks, :] = jnp.where(
        own > 0.0, jnp.log2(jnp.maximum(own, TINY)) - v, NEG
    )
    sums = jnp.concatenate(
        [jnp.sum(jnp.where(row_pair == k, f, 0.0), axis=0, keepdims=True) for k in range(pair_count)],
        axis=0,
    )
    sums = jnp.broadcast_to(jnp.sum(sums, axis=1, keepdims=True), (pair_count, LANES))
    y_box[0, y, pl.ds(col_blocks, 1), :] = jnp.sum(
        jnp.where(eye[:pair_count], sums, 0.0), axis=0, keepdims=True
    )
    with jax.named_scope("column_share_y"):
        share(
            y_box,
            0,
            y,
            size,
            [(in_y(r), tile) for r in sorted(range(1, NY), key=lambda r: -min(r, NY - r))],
            send_sem.at[1 + 2 * ITERS],
            y_sem,
        )
        z_box[0, z, :col_blocks, :] = merged(y_box[0, :, :col_blocks, :])
        z_box[0, z, pl.ds(col_blocks, 1), :] = jnp.sum(y_box[0, :, col_blocks:size, :], axis=0)
    with jax.named_scope("column_share_z"):
        share(
            z_box,
            0,
            z,
            size,
            [(in_z(r), tile) for r in sorted(range(1, nz), key=lambda r: -min(r, nz - r))],
            send_sem.at[2 + 2 * ITERS],
            z_sem,
        )
        v = log_rs - merged(z_box[0, :, :col_blocks, :])

    with jax.named_scope("results"):
        g_ref[...] = (EPS / LOG2E) * v + cn[...] * (1.0 / depth)
        sums = tall(jnp.sum(z_box[0, :, col_blocks:size, :], axis=0))
        value = jnp.zeros((2, LANES), jnp.float32)
        own_pair = jnp.zeros((2, LANES), jnp.int32)
        for t in range(TILES):
            value = jnp.where(tile == t, f[2 * t : 2 * t + 2], value)
            own_pair = jnp.where(tile == t, row_pair[2 * t : 2 * t + 2], own_pair)
        mean = jnp.zeros((2, LANES), jnp.float32)
        for k in range(pair_count):
            mean = jnp.where(own_pair == k, sums[k : k + 1, :], mean)
        f_ref[...] = value - mean / size_of(own_pair, row_sizes)

    with jax.named_scope("sent"):
        ref = rows.at[pl.ds(0, 7)]
        pltpu.make_async_copy(ref, ref, send_sem.at[0]).wait()
        for step in range(ITERS):
            width = row_box.shape[2] if step == 0 else halves
            sent(row_box, step, TILES - 1, width, send_sem.at[2 + step])
        for step in range(ITERS - 1):
            sent(near_box, step, len(near), col_blocks, send_sem.at[2 + ITERS + step])
        sent(y_box, 0, NY - 1, size, send_sem.at[1 + 2 * ITERS])
        sent(z_box, 0, nz - 1, size, send_sem.at[2 + 2 * ITERS])


def local(candidates, validation, row_sizes, col_sizes):
    groups = lax.axis_size("pair")
    n_row, depth = candidates.shape
    n_col = validation.shape[0]
    pairs = row_sizes.shape[0]
    halves = 2 * TILES
    half = n_row // 2
    col_blocks = n_col // LANES
    vmem = pl.BlockSpec(memory_space=pltpu.VMEM)
    whole = pl.BlockSpec(memory_space=pl.ANY)
    near = 2 * -(-ROW_MOST // (n_row * TILES))
    row_value, col_potential = pl.pallas_call(
        functools.partial(kernel, pairs, groups),
        out_shape=(
            jax.ShapeDtypeStruct((2, half), jnp.float32),
            jax.ShapeDtypeStruct((col_blocks, LANES), jnp.float32),
        ),
        in_specs=[whole] * 4,
        out_specs=(vmem, vmem),
        scratch_shapes=[
            pltpu.SMEM((pairs,), jnp.int32),
            pltpu.SMEM((pairs,), jnp.int32),
            pltpu.VMEM((n_col, depth), jnp.bfloat16),
            pltpu.VMEM((TILES, n_row, depth), jnp.bfloat16),
            pltpu.VMEM((n_col // 8, halves, 8, half), jnp.float32),
            pltpu.VMEM((n_col, LANES), jnp.float32),
            pltpu.VMEM((n_col, LANES), jnp.int32),
            pltpu.VMEM((n_col, LANES), jnp.float32),
            pltpu.VMEM((n_col, LANES), jnp.float32),
            pltpu.VMEM((col_blocks, LANES), jnp.float32),
            pltpu.VMEM((col_blocks, LANES), jnp.float32),
            pltpu.VMEM((ITERS, TILES, halves + 8, half), jnp.float32),
            pltpu.VMEM((ITERS - 1, near + 1, col_blocks, LANES), jnp.float32),
            pltpu.VMEM((1, NY, col_blocks + 8, LANES), jnp.float32),
            pltpu.VMEM((1, groups // NY, col_blocks + 8, LANES), jnp.float32),
            pltpu.SemaphoreType.DMA((4,)),
            pltpu.SemaphoreType.DMA((2 * ITERS + 3,)),
            pltpu.SemaphoreType.DMA((7, 2)),
            pltpu.SemaphoreType.REGULAR((HOPS,)),
            pltpu.SemaphoreType.DMA((ITERS,)),
            pltpu.SemaphoreType.DMA((ITERS - 1,)),
            pltpu.SemaphoreType.DMA,
            pltpu.SemaphoreType.DMA,
        ],
        compiler_params=pltpu.CompilerParams(
            collective_id=0, has_side_effects=True, vmem_limit_bytes=56 * 2**20
        ),
    )(row_sizes, col_sizes, candidates, validation)
    return row_value.reshape(n_row), col_potential.reshape(n_col)


def solution(mesh):
    in_specs = (P(("pair", "tile"), None), P("tile", None), P(), P())
    out_specs = (P(("pair", "tile")), P("tile"))
    return jax.shard_map(local, mesh=mesh, in_specs=in_specs, out_specs=out_specs, check_vma=False)
```

```python
import functools
import math

import jax
import jax.numpy as jnp
from jax import lax
from jax.experimental import pallas as pl
from jax.experimental.pallas import tpu as pltpu
from jax.sharding import PartitionSpec as P

ITERS = 3
EPS = 0.02
NEG = -1e30
EMPTY = -1e29
TINY = 1e-37
LOG2E = math.log2(math.e)
NX, NY = 4, 4
TILES = 2 * NX
ROW_MOST = 24576
HOPS = 4
TILE_ORDER = ((2, 0), (2, 1), (1, 1), (3, 1), (1, 0), (3, 0), (0, 1))
LANES = 128
MESH = pl.DeviceIdType.MESH


def pair_of(position, ends):
    pair = jnp.zeros(position.shape, jnp.int32)
    for end in ends:
        pair += (position >= end).astype(jnp.int32)
    return pair


def size_of(pair, sizes):
    size = jnp.zeros(pair.shape, jnp.float32)
    for k, s in enumerate(sizes):
        size = jnp.where(pair == k, s.astype(jnp.float32), size)
    return size


def merged(parts):
    top = jnp.max(parts, axis=0)
    return top + jnp.log2(jnp.sum(jnp.exp2(parts - top[None]), axis=0))


def kernel(
    pair_count,
    group_count,
    rs_hbm,
    cs_hbm,
    x_ref,
    y_hbm,
    f_ref,
    g_ref,
    rs_ref,
    cs_ref,
    y_ref,
    rows,
    scores,
    v_wide,
    pair_wide,
    top_wide,
    sum_wide,
    cn,
    column,
    row_box,
    near_box,
    y_box,
    z_box,
    local_sem,
    send_sem,
    block_sem,
    hop_sem,
    row_sem,
    near_sem,
    y_sem,
    z_sem,
):
    n_row, depth = x_ref.shape
    n_col = y_ref.shape[0]
    half = n_row // 2
    quarter = n_row // 4
    halves = 2 * TILES
    col_blocks = n_col // LANES
    nz = group_count // NY
    reach = -(-ROW_MOST // (n_row * TILES))
    scale = 2.0 * LOG2E / (depth * EPS)
    shift = LOG2E / (depth * EPS)

    group = lax.axis_index("pair")
    tile = lax.axis_index("tile")
    z, y = group // NY, lax.rem(group, NY)
    x, core = tile // 2, lax.rem(tile, 2)

    def at(dx, flip):
        other = 1 - core if flip else core
        return 2 * lax.rem(x + dx, NX) + other

    def in_y(r):
        return z * NY + lax.rem(y + r, NY)

    def in_z(r):
        return lax.rem(z + r, nz) * NY + y

    with jax.named_scope("greet"):
        offsets = sorted((r for r in range(-reach, reach + 1) if r), key=lambda r: -abs(r))
        near = [(lax.rem(group + r + group_count, group_count), tile) for r in offsets]
        neighbours = [(in_y(1), tile), (in_y(NY - 1), tile), (in_z(1), tile), (in_z(nz - 1), tile)]
        copies = [
            pltpu.make_async_copy(a, b, local_sem.at[i])
            for i, (a, b) in enumerate(
                [(x_ref, rows.at[tile]), (rs_hbm, rs_ref), (cs_hbm, cs_ref), (y_hbm, y_ref)]
            )
        ]
        for copy in copies:
            copy.start()
        barrier = pltpu.get_barrier_semaphore()
        for to in neighbours + [(group, at(dx, flip)) for dx, flip in ((1, 0), (NX - 1, 0), (0, 1))]:
            pl.semaphore_signal(barrier, device_id=to, device_id_type=MESH)
        copies[0].wait()
        pl.semaphore_wait(barrier, len(neighbours) + 3)

    def tell(r):
        for to in neighbours:
            pl.semaphore_signal(hop_sem.at[r - 1], device_id=to, device_id_type=MESH)

    def told(r):
        pl.semaphore_wait(hop_sem.at[r - 1], len(neighbours))

    def send(block, part, count, to, sem):
        ref = rows.at[block, pl.ds(part * quarter, count * quarter)]
        pltpu.make_async_remote_copy(
            src_ref=ref,
            dst_ref=ref,
            send_sem=send_sem.at[0],
            recv_sem=block_sem.at[sem, part],
            device_id=(group, to),
            device_id_type=MESH,
        ).start()

    def arrived(sem, part, count):
        ref = rows.at[0, pl.ds(0, count * quarter)]
        pltpu.make_async_copy(ref, ref, block_sem.at[sem, part]).wait()

    SIB, LEFT, RIGHT, LEFT_SIB, RIGHT_SIB, OPP, OPP_SIB = range(7)
    right, left, sib = at(1, False), at(NX - 1, False), at(0, True)

    with jax.named_scope("send_own"):
        for i in range(2):
            send(tile, i, 1, right, LEFT)
            send(tile, 3 - i, 1, left, RIGHT)
        send(tile, 0, 4, sib, SIB)
        tell(1)

    with jax.named_scope("inputs"):
        for copy in copies[1:]:
            copy.wait()

    row_ends, col_ends = [], []
    row_sizes, col_sizes = [], []
    for k in range(pair_count):
        row_sizes.append(rs_ref[k])
        col_sizes.append(cs_ref[k])
        row_ends.append(row_sizes[k] + (row_ends[-1] if k else 0))
        col_ends.append(col_sizes[k] + (col_ends[-1] if k else 0))

    lane = lax.broadcasted_iota(jnp.int32, (LANES, LANES), 1)
    line = lax.broadcasted_iota(jnp.int32, (LANES, LANES), 0)
    eye = lane == line

    def flat(tall):
        return jnp.sum(jnp.where(eye, tall, 0.0), axis=0, keepdims=True)

    def tall(flat_row):
        spread = jnp.where(eye, jnp.broadcast_to(flat_row, (LANES, LANES)), 0.0)
        return jnp.broadcast_to(jnp.sum(spread, axis=1, keepdims=True), (LANES, LANES))

    def squares(block):
        wide = block.astype(jnp.float32)
        total = jnp.sum(wide * wide, axis=1, keepdims=True)
        return jnp.broadcast_to(total, (LANES, LANES))

    with jax.named_scope("column_norms"):

        def column_block(q, carry):
            span = pl.ds(pl.multiple_of(q * LANES, LANES), LANES)
            norm = squares(y_ref[span, :])
            v_wide[span, :] = -shift * norm
            cn[pl.ds(q, 1), :] = flat(norm)
            pair_wide[span, :] = pair_of(tile * n_col + q * LANES + line, col_ends)
            return carry

        lax.fori_loop(0, col_blocks, column_block, 0)

    row_box[0, tile] = jnp.zeros(row_box.shape[2:], jnp.float32)
    for h in range(2):
        row_box[0, tile, pl.ds(halves + h, 1), :] = flat(
            squares(rows[tile, pl.ds(h * half, half), :])
        )

    chunk = min(1024, n_col)

    def score_block(block):
        first = group * (n_row * TILES) + block * n_row
        block_pair = [
            pair_of(first + h * half + lane[:1], row_ends) for h in range(2)
        ]

        def product(i, top):
            span = pl.ds(pl.multiple_of(i * chunk, chunk), chunk)
            cross = lax.dot_general(
                y_ref[span, :],
                rows[block],
                (((1,), (1,)), ((), ())),
                preferred_element_type=jnp.float32,
            )
            v = v_wide[span, :].reshape(chunk // 8, 8, LANES)
            col_pair = pair_wide[span, :]
            new = []
            for h in range(2):
                k = jnp.where(
                    col_pair == block_pair[h], cross[:, h * half : (h + 1) * half] * scale, NEG
                )
                k = k.reshape(chunk // 8, 8, LANES)
                scores[pl.ds(i * (chunk // 8), chunk // 8), 2 * block + h] = k
                new.append(jnp.maximum(top[h], jnp.max(k + v, axis=0)))
            return tuple(new)

        start = jnp.full((8, LANES), 4 * NEG, jnp.float32)
        top = lax.fori_loop(0, n_col // chunk, product, (start, start))
        top = [jnp.max(t, axis=0, keepdims=True) for t in top]

        def total(i, so_far):
            span = pl.ds(pl.multiple_of(i * LANES, LANES), LANES)
            v = v_wide[span, :].reshape(LANES // 8, 8, LANES)
            new = []
            for h in range(2):
                k = scores[pl.ds(i * (LANES // 8), LANES // 8), 2 * block + h]
                new.append(so_far[h] + jnp.sum(jnp.exp2(k + v - top[h][None]), axis=0))
            return tuple(new)

        start = jnp.zeros((8, LANES), jnp.float32)
        sums = lax.fori_loop(0, n_col // LANES, total, (start, start), unroll=4)
        for h in range(2):
            row_box[0, tile, pl.ds(2 * block + h, 1), :] = top[h] + jnp.log2(
                jnp.sum(sums[h], axis=0, keepdims=True)
            )

    def score_blocks(dx, flip):
        score_block(at(dx, flip))

    with jax.named_scope("scores_near"):
        score_blocks(0, False)
        send(tile, 2, 2, right, LEFT)
        send(tile, 0, 2, left, RIGHT)
        arrived(SIB, 0, 4)
        score_blocks(0, True)
        told(1)
        tell(2)

    left_block, right_block = at(NX - 1, False), at(1, False)
    opposite = at(2, False)
    with jax.named_scope("forward"):
        for i in range(2):
            arrived(LEFT, i, 1)
            send(left_block, i, 1, right, OPP)
            arrived(RIGHT, 3 - i, 1)
            send(right_block, 3 - i, 1, left, OPP)
        send(left_block, 0, 2, sib, LEFT_SIB)
        send(right_block, 2, 2, sib, RIGHT_SIB)
        arrived(LEFT, 2, 2)
        send(left_block, 2, 2, sib, LEFT_SIB)
        arrived(RIGHT, 0, 2)
        send(right_block, 0, 2, sib, RIGHT_SIB)
        told(2)
        tell(3)

    with jax.named_scope("scores_sides"):

        def side(s, carry):
            score_block(2 * lax.rem(x + 1 + 2 * s, NX) + core)
            return carry

        lax.fori_loop(0, 2, side, 0)
        for part in (0, 2):
            arrived(LEFT_SIB, part, 2)
            arrived(RIGHT_SIB, part, 2)

        def other_side(s, carry):
            score_block(2 * lax.rem(x + 1 + 2 * s, NX) + 1 - core)
            return carry

        lax.fori_loop(0, 2, other_side, 0)
        told(3)
        tell(4)

    with jax.named_scope("wait_opposite"):
        for part in (0, 3, 1, 2):
            arrived(OPP, part, 1)
            send(opposite, part, 1, sib, OPP_SIB)
    with jax.named_scope("scores_opposite"):
        score_blocks(2, False)
        for part in (0, 3, 1, 2):
            arrived(OPP_SIB, part, 1)
        score_blocks(2, True)

    row_line = lax.broadcasted_iota(jnp.int32, (halves, LANES), 0)
    row_lane = lax.broadcasted_iota(jnp.int32, (halves, LANES), 1)
    row_pair = pair_of(group * (n_row * TILES) + row_line * half + row_lane, row_ends)
    cs_of_row = size_of(row_pair, col_sizes)
    log_cs = jnp.log2(cs_of_row)
    col_line = lax.broadcasted_iota(jnp.int32, (col_blocks, LANES), 0)
    col_lane = lax.broadcasted_iota(jnp.int32, (col_blocks, LANES), 1)
    col_pair = pair_of(tile * n_col + col_line * LANES + col_lane, col_ends)
    rs_of_col = size_of(col_pair, row_sizes)
    log_rs = jnp.log2(rs_of_col)

    def row_sums():
        def add(i, so_far):
            span = pl.ds(pl.multiple_of(i * 8, 8), 8)
            return so_far + scores[i] * v_wide[span, :][None]

        start = jnp.zeros((halves, 8, LANES), jnp.float32)
        return jnp.sum(lax.fori_loop(0, n_col // 8, add, start, unroll=4), axis=1)

    def first_column_pass(u):
        u_wide = jnp.broadcast_to(u[:, None, :], (halves, 8, LANES))

        def lanes(i, carry):
            span = pl.ds(pl.multiple_of(i * 8, 8), 8)
            t = scores[i] + u_wide
            top = jnp.max(t, axis=0)
            e = jnp.exp2(t - top[None])
            scores[i] = e
            top_wide[span, :] = top
            sum_wide[span, :] = jnp.sum(e, axis=0)
            return carry

        lax.fori_loop(0, n_col // 8, lanes, 0, unroll=4)

        def across(q, carry):
            span = pl.ds(pl.multiple_of(q * LANES, LANES), LANES)
            tops = top_wide[span, :]
            top = jnp.max(tops, axis=1, keepdims=True)
            total = jnp.sum(sum_wide[span, :] * jnp.exp2(tops - top), axis=1, keepdims=True)
            wide = (LANES, LANES)
            column[pl.ds(q, 1), :] = flat(jnp.broadcast_to(top, wide)) + jnp.log2(
                flat(jnp.broadcast_to(total, wide))
            )
            return carry

        lax.fori_loop(0, col_blocks, across, 0, unroll=True)
        return column[...]

    def column_sums(b):
        b_wide = jnp.broadcast_to(b[:, None, :], (halves, 8, LANES))

        def lanes(i, carry):
            span = pl.ds(pl.multiple_of(i * 8, 8), 8)
            sum_wide[span, :] = jnp.sum(scores[i] * b_wide, axis=0) * top_wide[span, :]
            return carry

        lax.fori_loop(0, n_col // 8, lanes, 0, unroll=4)

        def across(q, carry):
            span = pl.ds(pl.multiple_of(q * LANES, LANES), LANES)
            total = jnp.sum(sum_wide[span, :], axis=1, keepdims=True)
            column[pl.ds(q, 1), :] = flat(jnp.broadcast_to(total, (LANES, LANES)))
            return carry

        lax.fori_loop(0, col_blocks, across, 0, unroll=True)
        return column[...]

    def share(box, step, me, size, targets, send, recv):
        own = box.at[step, len(targets) if me is None else me, pl.ds(0, size)]
        for i, to in enumerate(targets):
            pltpu.make_async_remote_copy(
                src_ref=own,
                dst_ref=box.at[step, i, pl.ds(0, size)] if me is None else own,
                send_sem=send,
                recv_sem=recv,
                device_id=to,
                device_id_type=MESH,
            ).start()
        some = box.at[step, pl.ds(0, len(targets)), pl.ds(0, size)]
        pltpu.make_async_copy(some, some, recv).wait()

    def sent(box, step, count, size, send):
        some = box.at[step, pl.ds(0, count), pl.ds(0, size)]
        pltpu.make_async_copy(some, some, send).wait()

    def share_rows(step):
        share(
            row_box,
            step,
            tile,
            row_box.shape[2] if step == 0 else halves,
            [(group, at(dx, flip)) for dx, flip in TILE_ORDER],
            send_sem.at[2 + step],
            row_sem.at[step],
        )
        return row_box[step, :, :halves, :]

    def share_columns(step, own):
        near_box[step, len(near)] = own
        share(
            near_box,
            step,
            None,
            col_blocks,
            near,
            send_sem.at[2 + ITERS + step],
            near_sem.at[step],
        )
        return near_box[step]

    with jax.named_scope("row_share"):
        u = log_cs - merged(share_rows(0))
    with jax.named_scope("column_pass"):
        column_lse = first_column_pass(u)
    told(HOPS)
    with jax.named_scope("column_share"):
        lse = merged(share_columns(0, column_lse))
        v = jnp.where(lse > EMPTY, log_rs - lse, 0.0)

    row_factor = jnp.ones((halves, LANES), jnp.float32)
    with jax.named_scope("spread"):
        for q in range(col_blocks):
            span = pl.ds(q * LANES, LANES)
            wide = jnp.exp2(top_wide[span, :] + tall(v[q : q + 1, :]))
            top_wide[span, :] = wide
            v_wide[span, :] = wide
    for step in range(1, ITERS):
        last = step + 1 == ITERS
        with jax.named_scope("row_pass"):
            row_box[step, tile, :halves, :] = row_sums()
        with jax.named_scope("row_share"):
            row_factor = cs_of_row / jnp.sum(share_rows(step), axis=0)
        with jax.named_scope("column_pass"):
            own = column_sums(row_factor)
        if not last:
            with jax.named_scope("column_share"):
                total = jnp.sum(share_columns(step, own), axis=0)
                factor = rs_of_col / jnp.maximum(total, 2.0**-60)
            with jax.named_scope("spread"):
                for q in range(col_blocks):
                    span = pl.ds(q * LANES, LANES)
                    v_wide[span, :] = top_wide[span, :] * tall(factor[q : q + 1, :])
    f = (EPS / LOG2E) * (u + jnp.log2(row_factor))
    f = f + jnp.concatenate(
        [row_box[0, t, halves : halves + 2, :] for t in range(TILES)], axis=0
    ) * (1.0 / depth)
    size = col_blocks + 1
    y_box[0, y, :col_blocks, :] = jnp.where(
        own > 0.0, jnp.log2(jnp.maximum(own, TINY)) - v, NEG
    )
    sums = jnp.concatenate(
        [jnp.sum(jnp.where(row_pair == k, f, 0.0), axis=0, keepdims=True) for k in range(pair_count)],
        axis=0,
    )
    sums = jnp.broadcast_to(jnp.sum(sums, axis=1, keepdims=True), (pair_count, LANES))
    y_box[0, y, pl.ds(col_blocks, 1), :] = jnp.sum(
        jnp.where(eye[:pair_count], sums, 0.0), axis=0, keepdims=True
    )
    with jax.named_scope("column_share_y"):
        share(
            y_box,
            0,
            y,
            size,
            [(in_y(r), tile) for r in sorted(range(1, NY), key=lambda r: -min(r, NY - r))],
            send_sem.at[1 + 2 * ITERS],
            y_sem,
        )
        z_box[0, z, :col_blocks, :] = merged(y_box[0, :, :col_blocks, :])
        z_box[0, z, pl.ds(col_blocks, 1), :] = jnp.sum(y_box[0, :, col_blocks:size, :], axis=0)
    with jax.named_scope("column_share_z"):
        share(
            z_box,
            0,
            z,
            size,
            [(in_z(r), tile) for r in sorted(range(1, nz), key=lambda r: -min(r, nz - r))],
            send_sem.at[2 + 2 * ITERS],
            z_sem,
        )
        v = log_rs - merged(z_box[0, :, :col_blocks, :])

    with jax.named_scope("results"):
        g_ref[...] = (EPS / LOG2E) * v + cn[...] * (1.0 / depth)
        sums = tall(jnp.sum(z_box[0, :, col_blocks:size, :], axis=0))
        value = jnp.zeros((2, LANES), jnp.float32)
        own_pair = jnp.zeros((2, LANES), jnp.int32)
        for t in range(TILES):
            value = jnp.where(tile == t, f[2 * t : 2 * t + 2], value)
            own_pair = jnp.where(tile == t, row_pair[2 * t : 2 * t + 2], own_pair)
        mean = jnp.zeros((2, LANES), jnp.float32)
        for k in range(pair_count):
            mean = jnp.where(own_pair == k, sums[k : k + 1, :], mean)
        f_ref[...] = value - mean / size_of(own_pair, row_sizes)

    with jax.named_scope("sent"):
        ref = rows.at[pl.ds(0, 7)]
        pltpu.make_async_copy(ref, ref, send_sem.at[0]).wait()
        for step in range(ITERS):
            width = row_box.shape[2] if step == 0 else halves
            sent(row_box, step, TILES - 1, width, send_sem.at[2 + step])
        for step in range(ITERS - 1):
            sent(near_box, step, len(near), col_blocks, send_sem.at[2 + ITERS + step])
        sent(y_box, 0, NY - 1, size, send_sem.at[1 + 2 * ITERS])
        sent(z_box, 0, nz - 1, size, send_sem.at[2 + 2 * ITERS])


def local(candidates, validation, row_sizes, col_sizes):
    groups = lax.axis_size("pair")
    n_row, depth = candidates.shape
    n_col = validation.shape[0]
    pairs = row_sizes.shape[0]
    halves = 2 * TILES
    half = n_row // 2
    col_blocks = n_col // LANES
    vmem = pl.BlockSpec(memory_space=pltpu.VMEM)
    whole = pl.BlockSpec(memory_space=pl.ANY)
    near = 2 * -(-ROW_MOST // (n_row * TILES))
    row_value, col_potential = pl.pallas_call(
        functools.partial(kernel, pairs, groups),
        out_shape=(
            jax.ShapeDtypeStruct((2, half), jnp.float32),
            jax.ShapeDtypeStruct((col_blocks, LANES), jnp.float32),
        ),
        in_specs=[whole] * 4,
        out_specs=(vmem, vmem),
        scratch_shapes=[
            pltpu.SMEM((pairs,), jnp.int32),
            pltpu.SMEM((pairs,), jnp.int32),
            pltpu.VMEM((n_col, depth), jnp.bfloat16),
            pltpu.VMEM((TILES, n_row, depth), jnp.bfloat16),
            pltpu.VMEM((n_col // 8, halves, 8, half), jnp.float32),
            pltpu.VMEM((n_col, LANES), jnp.float32),
            pltpu.VMEM((n_col, LANES), jnp.int32),
            pltpu.VMEM((n_col, LANES), jnp.float32),
            pltpu.VMEM((n_col, LANES), jnp.float32),
            pltpu.VMEM((col_blocks, LANES), jnp.float32),
            pltpu.VMEM((col_blocks, LANES), jnp.float32),
            pltpu.VMEM((ITERS, TILES, halves + 8, half), jnp.float32),
            pltpu.VMEM((ITERS - 1, near + 1, col_blocks, LANES), jnp.float32),
            pltpu.VMEM((1, NY, col_blocks + 8, LANES), jnp.float32),
            pltpu.VMEM((1, groups // NY, col_blocks + 8, LANES), jnp.float32),
            pltpu.SemaphoreType.DMA((4,)),
            pltpu.SemaphoreType.DMA((2 * ITERS + 3,)),
            pltpu.SemaphoreType.DMA((7, 4)),
            pltpu.SemaphoreType.REGULAR((HOPS,)),
            pltpu.SemaphoreType.DMA((ITERS,)),
            pltpu.SemaphoreType.DMA((ITERS - 1,)),
            pltpu.SemaphoreType.DMA,
            pltpu.SemaphoreType.DMA,
        ],
        compiler_params=pltpu.CompilerParams(
            collective_id=0, has_side_effects=True, vmem_limit_bytes=56 * 2**20
        ),
    )(row_sizes, col_sizes, candidates, validation)
    return row_value.reshape(n_row), col_potential.reshape(n_col)


def solution(mesh):
    in_specs = (P(("pair", "tile"), None), P("tile", None), P(), P())
    out_specs = (P(("pair", "tile")), P("tile"))
    return jax.shard_map(local, mesh=mesh, in_specs=in_specs, out_specs=out_specs, check_vma=False)
```

```python
import functools
import math

import jax
import jax.numpy as jnp
from jax import lax
from jax.experimental import pallas as pl
from jax.experimental.pallas import tpu as pltpu
from jax.sharding import PartitionSpec as P

ITERS = 3
EPS = 0.02
NEG = -1e30
EMPTY = -1e29
TINY = 1e-37
LOG2E = math.log2(math.e)
NX, NY = 4, 4
TILES = 2 * NX
ROW_MOST = 24576
HOPS = 4
TILE_ORDER = ((2, 0), (2, 1), (1, 1), (3, 1), (1, 0), (3, 0), (0, 1))
LANES = 128
MESH = pl.DeviceIdType.MESH


def pair_of(position, ends):
    pair = jnp.zeros(position.shape, jnp.int32)
    for end in ends:
        pair += (position >= end).astype(jnp.int32)
    return pair


def size_of(pair, sizes):
    size = jnp.zeros(pair.shape, jnp.float32)
    for k, s in enumerate(sizes):
        size = jnp.where(pair == k, s.astype(jnp.float32), size)
    return size


def merged(parts):
    top = jnp.max(parts, axis=0)
    return top + jnp.log2(jnp.sum(jnp.exp2(parts - top[None]), axis=0))


def kernel(
    pair_count,
    group_count,
    rs_hbm,
    cs_hbm,
    x_ref,
    y_hbm,
    f_ref,
    g_ref,
    rs_ref,
    cs_ref,
    y_ref,
    rows,
    scores,
    v_wide,
    pair_wide,
    top_wide,
    sum_wide,
    cn,
    column,
    row_box,
    near_box,
    y_box,
    z_box,
    local_sem,
    send_sem,
    block_sem,
    hop_sem,
    row_sem,
    near_sem,
    y_sem,
    z_sem,
):
    n_row, depth = x_ref.shape
    n_col = y_ref.shape[0]
    half = n_row // 2
    quarter = n_row // 4
    halves = 2 * TILES
    col_blocks = n_col // LANES
    nz = group_count // NY
    reach = -(-ROW_MOST // (n_row * TILES))
    scale = 2.0 * LOG2E / (depth * EPS)
    shift = LOG2E / (depth * EPS)

    group = lax.axis_index("pair")
    tile = lax.axis_index("tile")
    z, y = group // NY, lax.rem(group, NY)
    x, core = tile // 2, lax.rem(tile, 2)

    def at(dx, flip):
        other = 1 - core if flip else core
        return 2 * lax.rem(x + dx, NX) + other

    def in_y(r):
        return z * NY + lax.rem(y + r, NY)

    def in_z(r):
        return lax.rem(z + r, nz) * NY + y

    with jax.named_scope("greet"):
        offsets = sorted((r for r in range(-reach, reach + 1) if r), key=lambda r: -abs(r))
        near = [(lax.rem(group + r + group_count, group_count), tile) for r in offsets]
        neighbours = [(in_y(1), tile), (in_y(NY - 1), tile), (in_z(1), tile), (in_z(nz - 1), tile)]
        copies = [
            pltpu.make_async_copy(a, b, local_sem.at[i])
            for i, (a, b) in enumerate(
                [(x_ref, rows.at[tile]), (rs_hbm, rs_ref), (cs_hbm, cs_ref), (y_hbm, y_ref)]
            )
        ]
        for copy in copies:
            copy.start()
        barrier = pltpu.get_barrier_semaphore()
        for to in neighbours + [(group, at(dx, flip)) for dx, flip in ((1, 0), (NX - 1, 0), (0, 1))]:
            pl.semaphore_signal(barrier, device_id=to, device_id_type=MESH)
        copies[0].wait()
        pl.semaphore_wait(barrier, len(neighbours) + 3)

    def tell(r):
        for to in neighbours:
            pl.semaphore_signal(hop_sem.at[r - 1], device_id=to, device_id_type=MESH)

    def told(r):
        pl.semaphore_wait(hop_sem.at[r - 1], len(neighbours))

    def send(block, part, count, to, sem):
        ref = rows.at[block, pl.ds(part * quarter, count * quarter)]
        pltpu.make_async_remote_copy(
            src_ref=ref,
            dst_ref=ref,
            send_sem=send_sem.at[0],
            recv_sem=block_sem.at[sem, part],
            device_id=(group, to),
            device_id_type=MESH,
        ).start()

    def arrived(sem, part, count):
        ref = rows.at[0, pl.ds(0, count * quarter)]
        pltpu.make_async_copy(ref, ref, block_sem.at[sem, part]).wait()

    SIB, LEFT, RIGHT, LEFT_SIB, RIGHT_SIB, OPP, OPP_SIB = range(7)
    right, left, sib = at(1, False), at(NX - 1, False), at(0, True)

    with jax.named_scope("send_own"):
        for i in range(2):
            send(tile, i, 1, right, LEFT)
            send(tile, 3 - i, 1, left, RIGHT)
        send(tile, 0, 4, sib, SIB)
        tell(1)

    with jax.named_scope("inputs"):
        for copy in copies[1:]:
            copy.wait()

    row_ends, col_ends = [], []
    row_sizes, col_sizes = [], []
    for k in range(pair_count):
        row_sizes.append(rs_ref[k])
        col_sizes.append(cs_ref[k])
        row_ends.append(row_sizes[k] + (row_ends[-1] if k else 0))
        col_ends.append(col_sizes[k] + (col_ends[-1] if k else 0))

    lane = lax.broadcasted_iota(jnp.int32, (LANES, LANES), 1)
    line = lax.broadcasted_iota(jnp.int32, (LANES, LANES), 0)
    eye = lane == line

    def flat(tall):
        return jnp.sum(jnp.where(eye, tall, 0.0), axis=0, keepdims=True)

    def tall(flat_row):
        spread = jnp.where(eye, jnp.broadcast_to(flat_row, (LANES, LANES)), 0.0)
        return jnp.broadcast_to(jnp.sum(spread, axis=1, keepdims=True), (LANES, LANES))

    def squares(block):
        wide = block.astype(jnp.float32)
        total = jnp.sum(wide * wide, axis=1, keepdims=True)
        return jnp.broadcast_to(total, (LANES, LANES))

    with jax.named_scope("column_norms"):

        def column_block(q, carry):
            span = pl.ds(pl.multiple_of(q * LANES, LANES), LANES)
            norm = squares(y_ref[span, :])
            v_wide[span, :] = -shift * norm
            cn[pl.ds(q, 1), :] = flat(norm)
            pair_wide[span, :] = pair_of(tile * n_col + q * LANES + line, col_ends)
            return carry

        lax.fori_loop(0, col_blocks, column_block, 0)

    row_box[0, tile] = jnp.zeros(row_box.shape[2:], jnp.float32)
    for h in range(2):
        row_box[0, tile, pl.ds(halves + h, 1), :] = flat(
            squares(rows[tile, pl.ds(h * half, half), :])
        )

    chunk = min(1024, n_col)

    def score_block(block):
        first = group * (n_row * TILES) + block * n_row
        block_pair = [
            pair_of(first + h * half + lane[:1], row_ends) for h in range(2)
        ]

        def product(i, top):
            span = pl.ds(pl.multiple_of(i * chunk, chunk), chunk)
            cross = lax.dot_general(
                y_ref[span, :],
                rows[block],
                (((1,), (1,)), ((), ())),
                preferred_element_type=jnp.float32,
            )
            v = v_wide[span, :].reshape(chunk // 8, 8, LANES)
            col_pair = pair_wide[span, :]
            new = []
            for h in range(2):
                k = jnp.where(
                    col_pair == block_pair[h], cross[:, h * half : (h + 1) * half] * scale, NEG
                )
                k = k.reshape(chunk // 8, 8, LANES)
                scores[pl.ds(i * (chunk // 8), chunk // 8), 2 * block + h] = k
                new.append(jnp.maximum(top[h], jnp.max(k + v, axis=0)))
            return tuple(new)

        start = jnp.full((8, LANES), 4 * NEG, jnp.float32)
        top = lax.fori_loop(0, n_col // chunk, product, (start, start))
        top = [jnp.max(t, axis=0, keepdims=True) for t in top]

        def total(i, so_far):
            span = pl.ds(pl.multiple_of(i * LANES, LANES), LANES)
            v = v_wide[span, :].reshape(LANES // 8, 8, LANES)
            new = []
            for h in range(2):
                k = scores[pl.ds(i * (LANES // 8), LANES // 8), 2 * block + h]
                new.append(so_far[h] + jnp.sum(jnp.exp2(k + v - top[h][None]), axis=0))
            return tuple(new)

        start = jnp.zeros((8, LANES), jnp.float32)
        sums = lax.fori_loop(0, n_col // LANES, total, (start, start), unroll=4)
        for h in range(2):
            row_box[0, tile, pl.ds(2 * block + h, 1), :] = top[h] + jnp.log2(
                jnp.sum(sums[h], axis=0, keepdims=True)
            )

    def score_blocks(dx, flip):
        score_block(at(dx, flip))

    with jax.named_scope("scores_near"):
        score_blocks(0, False)
        send(tile, 2, 2, right, LEFT)
        send(tile, 0, 2, left, RIGHT)
        arrived(SIB, 0, 4)
        score_blocks(0, True)
        told(1)
        tell(2)

    left_block, right_block = at(NX - 1, False), at(1, False)
    opposite = at(2, False)
    with jax.named_scope("forward"):
        for i in range(2):
            arrived(LEFT, i, 1)
            send(left_block, i, 1, right, OPP)
            send(left_block, i, 1, sib, LEFT_SIB)
            arrived(RIGHT, 3 - i, 1)
            send(right_block, 3 - i, 1, left, OPP)
            send(right_block, 3 - i, 1, sib, RIGHT_SIB)
        arrived(LEFT, 2, 2)
        send(left_block, 2, 2, sib, LEFT_SIB)
        arrived(RIGHT, 0, 2)
        send(right_block, 0, 2, sib, RIGHT_SIB)
        told(2)
        tell(3)

    with jax.named_scope("scores_sides"):

        def side(s, carry):
            score_block(2 * lax.rem(x + 1 + 2 * s, NX) + core)
            return carry

        lax.fori_loop(0, 2, side, 0)
        for i in range(2):
            arrived(LEFT_SIB, i, 1)
            arrived(RIGHT_SIB, 3 - i, 1)
        arrived(LEFT_SIB, 2, 2)
        arrived(RIGHT_SIB, 0, 2)

        def other_side(s, carry):
            score_block(2 * lax.rem(x + 1 + 2 * s, NX) + 1 - core)
            return carry

        lax.fori_loop(0, 2, other_side, 0)
        told(3)
        tell(4)

    with jax.named_scope("wait_opposite"):
        for part in (0, 3, 1, 2):
            arrived(OPP, part, 1)
            send(opposite, part, 1, sib, OPP_SIB)
    with jax.named_scope("scores_opposite"):
        score_blocks(2, False)
        for part in (0, 3, 1, 2):
            arrived(OPP_SIB, part, 1)
        score_blocks(2, True)

    row_line = lax.broadcasted_iota(jnp.int32, (halves, LANES), 0)
    row_lane = lax.broadcasted_iota(jnp.int32, (halves, LANES), 1)
    row_pair = pair_of(group * (n_row * TILES) + row_line * half + row_lane, row_ends)
    cs_of_row = size_of(row_pair, col_sizes)
    log_cs = jnp.log2(cs_of_row)
    col_line = lax.broadcasted_iota(jnp.int32, (col_blocks, LANES), 0)
    col_lane = lax.broadcasted_iota(jnp.int32, (col_blocks, LANES), 1)
    col_pair = pair_of(tile * n_col + col_line * LANES + col_lane, col_ends)
    rs_of_col = size_of(col_pair, row_sizes)
    log_rs = jnp.log2(rs_of_col)

    def row_sums():
        def add(i, so_far):
            span = pl.ds(pl.multiple_of(i * 8, 8), 8)
            return so_far + scores[i] * v_wide[span, :][None]

        start = jnp.zeros((halves, 8, LANES), jnp.float32)
        return jnp.sum(lax.fori_loop(0, n_col // 8, add, start, unroll=16), axis=1)

    def first_column_pass(u):
        u_wide = jnp.broadcast_to(u[:, None, :], (halves, 8, LANES))

        def lanes(i, carry):
            span = pl.ds(pl.multiple_of(i * 8, 8), 8)
            t = scores[i] + u_wide
            top = jnp.max(t, axis=0)
            e = jnp.exp2(t - top[None])
            scores[i] = e
            top_wide[span, :] = top
            sum_wide[span, :] = jnp.sum(e, axis=0)
            return carry

        lax.fori_loop(0, n_col // 8, lanes, 0, unroll=4)

        def across(q, carry):
            span = pl.ds(pl.multiple_of(q * LANES, LANES), LANES)
            tops = top_wide[span, :]
            top = jnp.max(tops, axis=1, keepdims=True)
            total = jnp.sum(sum_wide[span, :] * jnp.exp2(tops - top), axis=1, keepdims=True)
            wide = (LANES, LANES)
            column[pl.ds(q, 1), :] = flat(jnp.broadcast_to(top, wide)) + jnp.log2(
                flat(jnp.broadcast_to(total, wide))
            )
            return carry

        lax.fori_loop(0, col_blocks, across, 0, unroll=True)
        return column[...]

    def column_sums(b):
        b_wide = jnp.broadcast_to(b[:, None, :], (halves, 8, LANES))

        def lanes(i, carry):
            span = pl.ds(pl.multiple_of(i * 8, 8), 8)
            sum_wide[span, :] = jnp.sum(scores[i] * b_wide, axis=0) * top_wide[span, :]
            return carry

        lax.fori_loop(0, n_col // 8, lanes, 0, unroll=16)

        def across(q, carry):
            span = pl.ds(pl.multiple_of(q * LANES, LANES), LANES)
            total = jnp.sum(sum_wide[span, :], axis=1, keepdims=True)
            column[pl.ds(q, 1), :] = flat(jnp.broadcast_to(total, (LANES, LANES)))
            return carry

        lax.fori_loop(0, col_blocks, across, 0, unroll=True)
        return column[...]

    def share(box, step, me, size, targets, send, recv):
        own = box.at[step, len(targets) if me is None else me, pl.ds(0, size)]
        for i, to in enumerate(targets):
            pltpu.make_async_remote_copy(
                src_ref=own,
                dst_ref=box.at[step, i, pl.ds(0, size)] if me is None else own,
                send_sem=send,
                recv_sem=recv,
                device_id=to,
                device_id_type=MESH,
            ).start()
        some = box.at[step, pl.ds(0, len(targets)), pl.ds(0, size)]
        pltpu.make_async_copy(some, some, recv).wait()

    def sent(box, step, count, size, send):
        some = box.at[step, pl.ds(0, count), pl.ds(0, size)]
        pltpu.make_async_copy(some, some, send).wait()

    def share_rows(step):
        share(
            row_box,
            step,
            tile,
            halves + 2 if step == 0 else halves,
            [(group, at(dx, flip)) for dx, flip in TILE_ORDER],
            send_sem.at[2 + step],
            row_sem.at[step],
        )
        return row_box[step, :, :halves, :]

    def share_columns(step, own):
        near_box[step, len(near)] = own
        share(
            near_box,
            step,
            None,
            col_blocks,
            near,
            send_sem.at[2 + ITERS + step],
            near_sem.at[step],
        )
        return near_box[step]

    with jax.named_scope("row_share"):
        u = log_cs - merged(share_rows(0))
    with jax.named_scope("column_pass"):
        column_lse = first_column_pass(u)
    told(HOPS)
    with jax.named_scope("column_share"):
        lse = merged(share_columns(0, column_lse))
        v = jnp.where(lse > EMPTY, log_rs - lse, 0.0)

    row_factor = jnp.ones((halves, LANES), jnp.float32)
    with jax.named_scope("spread"):
        for q in range(col_blocks):
            span = pl.ds(q * LANES, LANES)
            wide = jnp.exp2(top_wide[span, :] + tall(v[q : q + 1, :]))
            top_wide[span, :] = wide
            v_wide[span, :] = wide
    for step in range(1, ITERS):
        last = step + 1 == ITERS
        with jax.named_scope("row_pass"):
            row_box[step, tile, :halves, :] = row_sums()
        with jax.named_scope("row_share"):
            row_factor = cs_of_row / jnp.sum(share_rows(step), axis=0)
        with jax.named_scope("column_pass"):
            own = column_sums(row_factor)
        if not last:
            with jax.named_scope("column_share"):
                total = jnp.sum(share_columns(step, own), axis=0)
                factor = rs_of_col / jnp.maximum(total, 2.0**-60)
            with jax.named_scope("spread"):
                for q in range(col_blocks):
                    span = pl.ds(q * LANES, LANES)
                    v_wide[span, :] = top_wide[span, :] * tall(factor[q : q + 1, :])
    f = (EPS / LOG2E) * (u + jnp.log2(row_factor))
    f = f + jnp.concatenate(
        [row_box[0, t, halves : halves + 2, :] for t in range(TILES)], axis=0
    ) * (1.0 / depth)
    size = col_blocks + 1
    y_box[0, y, :col_blocks, :] = jnp.where(
        own > 0.0, jnp.log2(jnp.maximum(own, TINY)) - v, NEG
    )
    sums = jnp.concatenate(
        [jnp.sum(jnp.where(row_pair == k, f, 0.0), axis=0, keepdims=True) for k in range(pair_count)],
        axis=0,
    )
    sums = jnp.broadcast_to(jnp.sum(sums, axis=1, keepdims=True), (pair_count, LANES))
    y_box[0, y, pl.ds(col_blocks, 1), :] = jnp.sum(
        jnp.where(eye[:pair_count], sums, 0.0), axis=0, keepdims=True
    )
    with jax.named_scope("column_share_y"):
        share(
            y_box,
            0,
            y,
            size,
            [(in_y(r), tile) for r in sorted(range(1, NY), key=lambda r: -min(r, NY - r))],
            send_sem.at[1 + 2 * ITERS],
            y_sem,
        )
        z_box[0, z, :col_blocks, :] = merged(y_box[0, :, :col_blocks, :])
        z_box[0, z, pl.ds(col_blocks, 1), :] = jnp.sum(y_box[0, :, col_blocks:size, :], axis=0)
    with jax.named_scope("column_share_z"):
        share(
            z_box,
            0,
            z,
            size,
            [(in_z(r), tile) for r in sorted(range(1, nz), key=lambda r: -min(r, nz - r))],
            send_sem.at[2 + 2 * ITERS],
            z_sem,
        )
        v = log_rs - merged(z_box[0, :, :col_blocks, :])

    with jax.named_scope("results"):
        g_ref[...] = (EPS / LOG2E) * v + cn[...] * (1.0 / depth)
        sums = tall(jnp.sum(z_box[0, :, col_blocks:size, :], axis=0))
        value = jnp.zeros((2, LANES), jnp.float32)
        own_pair = jnp.zeros((2, LANES), jnp.int32)
        for t in range(TILES):
            value = jnp.where(tile == t, f[2 * t : 2 * t + 2], value)
            own_pair = jnp.where(tile == t, row_pair[2 * t : 2 * t + 2], own_pair)
        mean = jnp.zeros((2, LANES), jnp.float32)
        for k in range(pair_count):
            mean = jnp.where(own_pair == k, sums[k : k + 1, :], mean)
        f_ref[...] = value - mean / size_of(own_pair, row_sizes)

    with jax.named_scope("sent"):
        ref = rows.at[pl.ds(0, 7)]
        pltpu.make_async_copy(ref, ref, send_sem.at[0]).wait()
        for step in range(ITERS):
            width = halves + 2 if step == 0 else halves
            sent(row_box, step, TILES - 1, width, send_sem.at[2 + step])
        for step in range(ITERS - 1):
            sent(near_box, step, len(near), col_blocks, send_sem.at[2 + ITERS + step])
        sent(y_box, 0, NY - 1, size, send_sem.at[1 + 2 * ITERS])
        sent(z_box, 0, nz - 1, size, send_sem.at[2 + 2 * ITERS])


def local(candidates, validation, row_sizes, col_sizes):
    groups = lax.axis_size("pair")
    n_row, depth = candidates.shape
    n_col = validation.shape[0]
    pairs = row_sizes.shape[0]
    halves = 2 * TILES
    half = n_row // 2
    col_blocks = n_col // LANES
    vmem = pl.BlockSpec(memory_space=pltpu.VMEM)
    whole = pl.BlockSpec(memory_space=pl.ANY)
    near = 2 * -(-ROW_MOST // (n_row * TILES))
    row_value, col_potential = pl.pallas_call(
        functools.partial(kernel, pairs, groups),
        out_shape=(
            jax.ShapeDtypeStruct((2, half), jnp.float32),
            jax.ShapeDtypeStruct((col_blocks, LANES), jnp.float32),
        ),
        in_specs=[whole] * 4,
        out_specs=(vmem, vmem),
        scratch_shapes=[
            pltpu.SMEM((pairs,), jnp.int32),
            pltpu.SMEM((pairs,), jnp.int32),
            pltpu.VMEM((n_col, depth), jnp.bfloat16),
            pltpu.VMEM((TILES, n_row, depth), jnp.bfloat16),
            pltpu.VMEM((n_col // 8, halves, 8, half), jnp.float32),
            pltpu.VMEM((n_col, LANES), jnp.float32),
            pltpu.VMEM((n_col, LANES), jnp.int32),
            pltpu.VMEM((n_col, LANES), jnp.float32),
            pltpu.VMEM((n_col, LANES), jnp.float32),
            pltpu.VMEM((col_blocks, LANES), jnp.float32),
            pltpu.VMEM((col_blocks, LANES), jnp.float32),
            pltpu.VMEM((ITERS, TILES, halves + 8, half), jnp.float32),
            pltpu.VMEM((ITERS - 1, near + 1, col_blocks, LANES), jnp.float32),
            pltpu.VMEM((1, NY, col_blocks + 8, LANES), jnp.float32),
            pltpu.VMEM((1, groups // NY, col_blocks + 8, LANES), jnp.float32),
            pltpu.SemaphoreType.DMA((4,)),
            pltpu.SemaphoreType.DMA((2 * ITERS + 3,)),
            pltpu.SemaphoreType.DMA((7, 4)),
            pltpu.SemaphoreType.REGULAR((HOPS,)),
            pltpu.SemaphoreType.DMA((ITERS,)),
            pltpu.SemaphoreType.DMA((ITERS - 1,)),
            pltpu.SemaphoreType.DMA,
            pltpu.SemaphoreType.DMA,
        ],
        compiler_params=pltpu.CompilerParams(
            collective_id=0, has_side_effects=True, vmem_limit_bytes=56 * 2**20
        ),
    )(row_sizes, col_sizes, candidates, validation)
    return row_value.reshape(n_row), col_potential.reshape(n_col)


def solution(mesh):
    in_specs = (P(("pair", "tile"), None), P("tile", None), P(), P())
    out_specs = (P(("pair", "tile")), P("tile"))
    return jax.shard_map(local, mesh=mesh, in_specs=in_specs, out_specs=out_specs, check_vma=False)
```

```python
import functools
import math

import jax
import jax.numpy as jnp
from jax import lax
from jax.experimental import pallas as pl
from jax.experimental.pallas import tpu as pltpu
from jax.sharding import PartitionSpec as P

ITERS = 3
EPS = 0.02
NEG = -1e30
EMPTY = -1e29
TINY = 1e-37
LOG2E = math.log2(math.e)
NX, NY = 4, 4
TILES = 2 * NX
ROW_MOST = 24576
HOPS = 4
TILE_ORDER = ((2, 0), (2, 1), (1, 1), (3, 1), (1, 0), (3, 0), (0, 1))
LANES = 128
MESH = pl.DeviceIdType.MESH


def pair_of(position, ends):
    pair = jnp.zeros(position.shape, jnp.int32)
    for end in ends:
        pair += (position >= end).astype(jnp.int32)
    return pair


def size_of(pair, sizes):
    size = jnp.zeros(pair.shape, jnp.float32)
    for k, s in enumerate(sizes):
        size = jnp.where(pair == k, s.astype(jnp.float32), size)
    return size


def merged(parts):
    top = jnp.max(parts, axis=0)
    return top + jnp.log2(jnp.sum(jnp.exp2(parts - top[None]), axis=0))


def kernel(
    pair_count,
    group_count,
    rs_hbm,
    cs_hbm,
    x_ref,
    y_hbm,
    f_ref,
    g_ref,
    rs_ref,
    cs_ref,
    y_ref,
    rows,
    scores,
    v_wide,
    pair_wide,
    top_wide,
    sum_wide,
    cn,
    column,
    row_box,
    near_box,
    y_box,
    z_box,
    local_sem,
    send_sem,
    block_sem,
    hop_sem,
    row_sem,
    near_sem,
    y_sem,
    sum_sem,
    z_sem,
):
    n_row, depth = x_ref.shape
    n_col = y_ref.shape[0]
    half = n_row // 2
    quarter = n_row // 4
    halves = 2 * TILES
    col_blocks = n_col // LANES
    nz = group_count // NY
    reach = -(-ROW_MOST // (n_row * TILES))
    scale = 2.0 * LOG2E / (depth * EPS)
    shift = LOG2E / (depth * EPS)

    group = lax.axis_index("pair")
    tile = lax.axis_index("tile")
    z, y = group // NY, lax.rem(group, NY)
    x, core = tile // 2, lax.rem(tile, 2)

    def at(dx, flip):
        other = 1 - core if flip else core
        return 2 * lax.rem(x + dx, NX) + other

    def in_y(r):
        return z * NY + lax.rem(y + r, NY)

    def in_z(r):
        return lax.rem(z + r, nz) * NY + y

    with jax.named_scope("greet"):
        offsets = sorted((r for r in range(-reach, reach + 1) if r), key=lambda r: -abs(r))
        near = [(lax.rem(group + r + group_count, group_count), tile) for r in offsets]
        neighbours = [(in_y(1), tile), (in_y(NY - 1), tile), (in_z(1), tile), (in_z(nz - 1), tile)]
        copies = [
            pltpu.make_async_copy(a, b, local_sem.at[i])
            for i, (a, b) in enumerate(
                [(x_ref, rows.at[tile]), (rs_hbm, rs_ref), (cs_hbm, cs_ref), (y_hbm, y_ref)]
            )
        ]
        for copy in copies:
            copy.start()
        barrier = pltpu.get_barrier_semaphore()
        for to in neighbours + [(group, at(dx, flip)) for dx, flip in ((1, 0), (NX - 1, 0), (0, 1))]:
            pl.semaphore_signal(barrier, device_id=to, device_id_type=MESH)
        copies[0].wait()
        pl.semaphore_wait(barrier, len(neighbours) + 3)

    def tell(r):
        for to in neighbours:
            pl.semaphore_signal(hop_sem.at[r - 1], device_id=to, device_id_type=MESH)

    def told(r):
        pl.semaphore_wait(hop_sem.at[r - 1], len(neighbours))

    def send(block, part, count, to, sem):
        ref = rows.at[block, pl.ds(part * quarter, count * quarter)]
        pltpu.make_async_remote_copy(
            src_ref=ref,
            dst_ref=ref,
            send_sem=send_sem.at[0],
            recv_sem=block_sem.at[sem, part],
            device_id=(group, to),
            device_id_type=MESH,
        ).start()

    def arrived(sem, part, count):
        ref = rows.at[0, pl.ds(0, count * quarter)]
        pltpu.make_async_copy(ref, ref, block_sem.at[sem, part]).wait()

    SIB, LEFT, RIGHT, LEFT_SIB, RIGHT_SIB, OPP, OPP_SIB = range(7)
    right, left, sib = at(1, False), at(NX - 1, False), at(0, True)

    with jax.named_scope("send_own"):
        for i in range(2):
            send(tile, i, 1, right, LEFT)
            send(tile, 3 - i, 1, left, RIGHT)
        send(tile, 0, 4, sib, SIB)
        tell(1)

    with jax.named_scope("inputs"):
        for copy in copies[1:]:
            copy.wait()

    row_ends, col_ends = [], []
    row_sizes, col_sizes = [], []
    for k in range(pair_count):
        row_sizes.append(rs_ref[k])
        col_sizes.append(cs_ref[k])
        row_ends.append(row_sizes[k] + (row_ends[-1] if k else 0))
        col_ends.append(col_sizes[k] + (col_ends[-1] if k else 0))

    lane = lax.broadcasted_iota(jnp.int32, (LANES, LANES), 1)
    line = lax.broadcasted_iota(jnp.int32, (LANES, LANES), 0)
    eye = lane == line

    def flat(tall):
        return jnp.sum(jnp.where(eye, tall, 0.0), axis=0, keepdims=True)

    def tall(flat_row):
        spread = jnp.where(eye, jnp.broadcast_to(flat_row, (LANES, LANES)), 0.0)
        return jnp.broadcast_to(jnp.sum(spread, axis=1, keepdims=True), (LANES, LANES))

    def squares(block):
        wide = block.astype(jnp.float32)
        total = jnp.sum(wide * wide, axis=1, keepdims=True)
        return jnp.broadcast_to(total, (LANES, LANES))

    with jax.named_scope("column_norms"):

        def column_block(q, carry):
            span = pl.ds(pl.multiple_of(q * LANES, LANES), LANES)
            norm = squares(y_ref[span, :])
            v_wide[span, :] = -shift * norm
            cn[pl.ds(q, 1), :] = flat(norm)
            pair_wide[span, :] = pair_of(tile * n_col + q * LANES + line, col_ends)
            return carry

        lax.fori_loop(0, col_blocks, column_block, 0)

    row_box[0, tile] = jnp.zeros(row_box.shape[2:], jnp.float32)
    for h in range(2):
        row_box[0, tile, pl.ds(halves + h, 1), :] = flat(
            squares(rows[tile, pl.ds(h * half, half), :])
        )

    chunk = min(1024, n_col)

    def score_block(block):
        first = group * (n_row * TILES) + block * n_row
        block_pair = [
            pair_of(first + h * half + lane[:1], row_ends) for h in range(2)
        ]

        def product(i, top):
            span = pl.ds(pl.multiple_of(i * chunk, chunk), chunk)
            cross = lax.dot_general(
                y_ref[span, :],
                rows[block],
                (((1,), (1,)), ((), ())),
                preferred_element_type=jnp.float32,
            )
            v = v_wide[span, :].reshape(chunk // 8, 8, LANES)
            col_pair = pair_wide[span, :]
            new = []
            for h in range(2):
                k = jnp.where(
                    col_pair == block_pair[h], cross[:, h * half : (h + 1) * half] * scale, NEG
                )
                k = k.reshape(chunk // 8, 8, LANES)
                scores[pl.ds(i * (chunk // 8), chunk // 8), 2 * block + h] = k
                new.append(jnp.maximum(top[h], jnp.max(k + v, axis=0)))
            return tuple(new)

        start = jnp.full((8, LANES), 4 * NEG, jnp.float32)
        top = lax.fori_loop(0, n_col // chunk, product, (start, start))
        top = [jnp.max(t, axis=0, keepdims=True) for t in top]

        def total(i, so_far):
            span = pl.ds(pl.multiple_of(i * LANES, LANES), LANES)
            v = v_wide[span, :].reshape(LANES // 8, 8, LANES)
            new = []
            for h in range(2):
                k = scores[pl.ds(i * (LANES // 8), LANES // 8), 2 * block + h]
                new.append(so_far[h] + jnp.sum(jnp.exp2(k + v - top[h][None]), axis=0))
            return tuple(new)

        start = jnp.zeros((8, LANES), jnp.float32)
        sums = lax.fori_loop(0, n_col // LANES, total, (start, start), unroll=4)
        for h in range(2):
            row_box[0, tile, pl.ds(2 * block + h, 1), :] = top[h] + jnp.log2(
                jnp.sum(sums[h], axis=0, keepdims=True)
            )

    def score_blocks(dx, flip):
        score_block(at(dx, flip))

    with jax.named_scope("scores_near"):
        score_blocks(0, False)
        send(tile, 2, 2, right, LEFT)
        send(tile, 0, 2, left, RIGHT)
        arrived(SIB, 0, 4)
        score_blocks(0, True)
        told(1)
        tell(2)

    left_block, right_block = at(NX - 1, False), at(1, False)
    opposite = at(2, False)
    with jax.named_scope("forward"):
        for i in range(2):
            arrived(LEFT, i, 1)
            send(left_block, i, 1, right, OPP)
            send(left_block, i, 1, sib, LEFT_SIB)
            arrived(RIGHT, 3 - i, 1)
            send(right_block, 3 - i, 1, left, OPP)
            send(right_block, 3 - i, 1, sib, RIGHT_SIB)
        arrived(LEFT, 2, 2)
        send(left_block, 2, 2, sib, LEFT_SIB)
        arrived(RIGHT, 0, 2)
        send(right_block, 0, 2, sib, RIGHT_SIB)
        told(2)
        tell(3)

    with jax.named_scope("scores_sides"):

        def side(s, carry):
            score_block(2 * lax.rem(x + 1 + 2 * s, NX) + core)
            return carry

        lax.fori_loop(0, 2, side, 0)
        for i in range(2):
            arrived(LEFT_SIB, i, 1)
            arrived(RIGHT_SIB, 3 - i, 1)
        arrived(LEFT_SIB, 2, 2)
        arrived(RIGHT_SIB, 0, 2)

        def other_side(s, carry):
            score_block(2 * lax.rem(x + 1 + 2 * s, NX) + 1 - core)
            return carry

        lax.fori_loop(0, 2, other_side, 0)
        told(3)
        tell(4)

    with jax.named_scope("wait_opposite"):
        for part in (0, 3, 1, 2):
            arrived(OPP, part, 1)
            send(opposite, part, 1, sib, OPP_SIB)
    with jax.named_scope("scores_opposite"):
        score_blocks(2, False)
        for part in (0, 3, 1, 2):
            arrived(OPP_SIB, part, 1)
        score_blocks(2, True)

    row_line = lax.broadcasted_iota(jnp.int32, (halves, LANES), 0)
    row_lane = lax.broadcasted_iota(jnp.int32, (halves, LANES), 1)
    row_pair = pair_of(group * (n_row * TILES) + row_line * half + row_lane, row_ends)
    cs_of_row = size_of(row_pair, col_sizes)
    log_cs = jnp.log2(cs_of_row)
    col_line = lax.broadcasted_iota(jnp.int32, (col_blocks, LANES), 0)
    col_lane = lax.broadcasted_iota(jnp.int32, (col_blocks, LANES), 1)
    col_pair = pair_of(tile * n_col + col_line * LANES + col_lane, col_ends)
    rs_of_col = size_of(col_pair, row_sizes)
    log_rs = jnp.log2(rs_of_col)

    def row_sums():
        def add(i, so_far):
            span = pl.ds(pl.multiple_of(i * 8, 8), 8)
            return so_far + scores[i] * v_wide[span, :][None]

        start = jnp.zeros((halves, 8, LANES), jnp.float32)
        return jnp.sum(lax.fori_loop(0, n_col // 8, add, start, unroll=16), axis=1)

    def first_column_pass(u):
        u_wide = jnp.broadcast_to(u[:, None, :], (halves, 8, LANES))

        def lanes(i, carry):
            span = pl.ds(pl.multiple_of(i * 8, 8), 8)
            t = scores[i] + u_wide
            top = jnp.max(t, axis=0)
            e = jnp.exp2(t - top[None])
            scores[i] = e
            top_wide[span, :] = top
            sum_wide[span, :] = jnp.sum(e, axis=0)
            return carry

        lax.fori_loop(0, n_col // 8, lanes, 0, unroll=4)

        def across(q, carry):
            span = pl.ds(pl.multiple_of(q * LANES, LANES), LANES)
            tops = top_wide[span, :]
            top = jnp.max(tops, axis=1, keepdims=True)
            total = jnp.sum(sum_wide[span, :] * jnp.exp2(tops - top), axis=1, keepdims=True)
            wide = (LANES, LANES)
            column[pl.ds(q, 1), :] = flat(jnp.broadcast_to(top, wide)) + jnp.log2(
                flat(jnp.broadcast_to(total, wide))
            )
            return carry

        lax.fori_loop(0, col_blocks, across, 0, unroll=True)
        return column[...]

    def column_sums(b):
        b_wide = jnp.broadcast_to(b[:, None, :], (halves, 8, LANES))

        def lanes(i, carry):
            span = pl.ds(pl.multiple_of(i * 8, 8), 8)
            sum_wide[span, :] = jnp.sum(scores[i] * b_wide, axis=0) * top_wide[span, :]
            return carry

        lax.fori_loop(0, n_col // 8, lanes, 0, unroll=16)

        def across(q, carry):
            span = pl.ds(pl.multiple_of(q * LANES, LANES), LANES)
            total = jnp.sum(sum_wide[span, :], axis=1, keepdims=True)
            column[pl.ds(q, 1), :] = flat(jnp.broadcast_to(total, (LANES, LANES)))
            return carry

        lax.fori_loop(0, col_blocks, across, 0, unroll=True)
        return column[...]

    def share(box, step, me, size, targets, send, recv, meanwhile=lambda: None):
        own = box.at[step, len(targets) if me is None else me, pl.ds(0, size)]
        for i, to in enumerate(targets):
            pltpu.make_async_remote_copy(
                src_ref=own,
                dst_ref=box.at[step, i, pl.ds(0, size)] if me is None else own,
                send_sem=send,
                recv_sem=recv,
                device_id=to,
                device_id_type=MESH,
            ).start()
        made = meanwhile()
        some = box.at[step, pl.ds(0, len(targets)), pl.ds(0, size)]
        pltpu.make_async_copy(some, some, recv).wait()
        return made

    def sent(box, step, count, size, send):
        some = box.at[step, pl.ds(0, count), pl.ds(0, size)]
        pltpu.make_async_copy(some, some, send).wait()

    def share_rows(step):
        share(
            row_box,
            step,
            tile,
            halves + 2 if step == 0 else halves,
            [(group, at(dx, flip)) for dx, flip in TILE_ORDER],
            send_sem.at[2 + step],
            row_sem.at[step],
        )
        return row_box[step, :, :halves, :]

    def share_columns(step, own):
        near_box[step, len(near)] = own
        share(
            near_box,
            step,
            None,
            col_blocks,
            near,
            send_sem.at[2 + ITERS + step],
            near_sem.at[step],
        )
        return near_box[step]

    with jax.named_scope("row_share"):
        u = log_cs - merged(share_rows(0))
    with jax.named_scope("column_pass"):
        column_lse = first_column_pass(u)
    told(HOPS)
    with jax.named_scope("column_share"):
        lse = merged(share_columns(0, column_lse))
        v = jnp.where(lse > EMPTY, log_rs - lse, 0.0)

    row_factor = jnp.ones((halves, LANES), jnp.float32)
    with jax.named_scope("spread"):
        for q in range(col_blocks):
            span = pl.ds(q * LANES, LANES)
            wide = jnp.exp2(top_wide[span, :] + tall(v[q : q + 1, :]))
            top_wide[span, :] = wide
            v_wide[span, :] = wide
    for step in range(1, ITERS):
        last = step + 1 == ITERS
        with jax.named_scope("row_pass"):
            row_box[step, tile, :halves, :] = row_sums()
        with jax.named_scope("row_share"):
            row_factor = cs_of_row / jnp.sum(share_rows(step), axis=0)
        with jax.named_scope("column_pass"):
            own = column_sums(row_factor)
        if not last:
            with jax.named_scope("column_share"):
                total = jnp.sum(share_columns(step, own), axis=0)
                factor = rs_of_col / jnp.maximum(total, 2.0**-60)
            with jax.named_scope("spread"):
                for q in range(col_blocks):
                    span = pl.ds(q * LANES, LANES)
                    v_wide[span, :] = top_wide[span, :] * tall(factor[q : q + 1, :])
    size = col_blocks + 1
    y_box[0, y, :col_blocks, :] = jnp.where(
        own > 0.0, jnp.log2(jnp.maximum(own, TINY)) - v, NEG
    )
    y_targets = [(in_y(r), tile) for r in sorted(range(1, NY), key=lambda r: -min(r, NY - r))]

    def pair_sums():
        f = (EPS / LOG2E) * (u + jnp.log2(row_factor))
        f = f + jnp.concatenate(
            [row_box[0, t, halves : halves + 2, :] for t in range(TILES)], axis=0
        ) * (1.0 / depth)
        sums = jnp.concatenate(
            [jnp.sum(jnp.where(row_pair == k, f, 0.0), axis=0, keepdims=True) for k in range(pair_count)],
            axis=0,
        )
        sums = jnp.broadcast_to(jnp.sum(sums, axis=1, keepdims=True), (pair_count, LANES))
        y_box[0, y, pl.ds(col_blocks, 1), :] = jnp.sum(
            jnp.where(eye[:pair_count], sums, 0.0), axis=0, keepdims=True
        )
        mine = y_box.at[0, y, pl.ds(col_blocks, 1)]
        for to in y_targets:
            pltpu.make_async_remote_copy(
                src_ref=mine,
                dst_ref=mine,
                send_sem=send_sem.at[1],
                recv_sem=sum_sem,
                device_id=to,
                device_id_type=MESH,
            ).start()
        return f

    with jax.named_scope("column_share_y"):
        f = share(
            y_box,
            0,
            y,
            col_blocks,
            y_targets,
            send_sem.at[1 + 2 * ITERS],
            y_sem,
            pair_sums,
        )
        some = y_box.at[0, pl.ds(0, NY - 1), pl.ds(col_blocks, 1)]
        pltpu.make_async_copy(some, some, sum_sem).wait()
        z_box[0, z, :col_blocks, :] = merged(y_box[0, :, :col_blocks, :])
        z_box[0, z, pl.ds(col_blocks, 1), :] = jnp.sum(y_box[0, :, col_blocks:size, :], axis=0)
    with jax.named_scope("column_share_z"):
        share(
            z_box,
            0,
            z,
            size,
            [(in_z(r), tile) for r in sorted(range(1, nz), key=lambda r: -min(r, nz - r))],
            send_sem.at[2 + 2 * ITERS],
            z_sem,
        )
        v = log_rs - merged(z_box[0, :, :col_blocks, :])

    with jax.named_scope("results"):
        g_ref[...] = (EPS / LOG2E) * v + cn[...] * (1.0 / depth)
        sums = tall(jnp.sum(z_box[0, :, col_blocks:size, :], axis=0))
        value = jnp.zeros((2, LANES), jnp.float32)
        own_pair = jnp.zeros((2, LANES), jnp.int32)
        for t in range(TILES):
            value = jnp.where(tile == t, f[2 * t : 2 * t + 2], value)
            own_pair = jnp.where(tile == t, row_pair[2 * t : 2 * t + 2], own_pair)
        mean = jnp.zeros((2, LANES), jnp.float32)
        for k in range(pair_count):
            mean = jnp.where(own_pair == k, sums[k : k + 1, :], mean)
        f_ref[...] = value - mean / size_of(own_pair, row_sizes)

    with jax.named_scope("sent"):
        ref = rows.at[pl.ds(0, 7)]
        pltpu.make_async_copy(ref, ref, send_sem.at[0]).wait()
        for step in range(ITERS):
            width = halves + 2 if step == 0 else halves
            sent(row_box, step, TILES - 1, width, send_sem.at[2 + step])
        for step in range(ITERS - 1):
            sent(near_box, step, len(near), col_blocks, send_sem.at[2 + ITERS + step])
        sent(y_box, 0, NY - 1, col_blocks, send_sem.at[1 + 2 * ITERS])
        pltpu.make_async_copy(some, some, send_sem.at[1]).wait()
        sent(z_box, 0, nz - 1, size, send_sem.at[2 + 2 * ITERS])


def local(candidates, validation, row_sizes, col_sizes):
    groups = lax.axis_size("pair")
    n_row, depth = candidates.shape
    n_col = validation.shape[0]
    pairs = row_sizes.shape[0]
    halves = 2 * TILES
    half = n_row // 2
    col_blocks = n_col // LANES
    vmem = pl.BlockSpec(memory_space=pltpu.VMEM)
    whole = pl.BlockSpec(memory_space=pl.ANY)
    near = 2 * -(-ROW_MOST // (n_row * TILES))
    row_value, col_potential = pl.pallas_call(
        functools.partial(kernel, pairs, groups),
        out_shape=(
            jax.ShapeDtypeStruct((2, half), jnp.float32),
            jax.ShapeDtypeStruct((col_blocks, LANES), jnp.float32),
        ),
        in_specs=[whole] * 4,
        out_specs=(vmem, vmem),
        scratch_shapes=[
            pltpu.SMEM((pairs,), jnp.int32),
            pltpu.SMEM((pairs,), jnp.int32),
            pltpu.VMEM((n_col, depth), jnp.bfloat16),
            pltpu.VMEM((TILES, n_row, depth), jnp.bfloat16),
            pltpu.VMEM((n_col // 8, halves, 8, half), jnp.float32),
            pltpu.VMEM((n_col, LANES), jnp.float32),
            pltpu.VMEM((n_col, LANES), jnp.int32),
            pltpu.VMEM((n_col, LANES), jnp.float32),
            pltpu.VMEM((n_col, LANES), jnp.float32),
            pltpu.VMEM((col_blocks, LANES), jnp.float32),
            pltpu.VMEM((col_blocks, LANES), jnp.float32),
            pltpu.VMEM((ITERS, TILES, halves + 8, half), jnp.float32),
            pltpu.VMEM((ITERS - 1, near + 1, col_blocks, LANES), jnp.float32),
            pltpu.VMEM((1, NY, col_blocks + 8, LANES), jnp.float32),
            pltpu.VMEM((1, groups // NY, col_blocks + 8, LANES), jnp.float32),
            pltpu.SemaphoreType.DMA((4,)),
            pltpu.SemaphoreType.DMA((2 * ITERS + 3,)),
            pltpu.SemaphoreType.DMA((7, 4)),
            pltpu.SemaphoreType.REGULAR((HOPS,)),
            pltpu.SemaphoreType.DMA((ITERS,)),
            pltpu.SemaphoreType.DMA((ITERS - 1,)),
            pltpu.SemaphoreType.DMA,
            pltpu.SemaphoreType.DMA,
            pltpu.SemaphoreType.DMA,
        ],
        compiler_params=pltpu.CompilerParams(
            collective_id=0, has_side_effects=True, vmem_limit_bytes=56 * 2**20
        ),
    )(row_sizes, col_sizes, candidates, validation)
    return row_value.reshape(n_row), col_potential.reshape(n_col)


def solution(mesh):
    in_specs = (P(("pair", "tile"), None), P("tile", None), P(), P())
    out_specs = (P(("pair", "tile")), P("tile"))
    return jax.shard_map(local, mesh=mesh, in_specs=in_specs, out_specs=out_specs, check_vma=False)
```
